32 devices in a mesh: tp: 4 (over y, x), lat: 8 (over z, core).
Axes of the slice: x: 2, y: 2, z: 4, core: 2. Of those that a mesh axis runs over, the one named last changes fastest.
Arguments:
- attn_out: bfloat16 [512, 2048], P('lat', 'tp'), may hold values from -6 to 6
- w_out: bfloat16 [2048, 8192], P('tp'), may hold values from -0.125 to 0.125
- resid_in: bfloat16 [512, 8192], P(('lat', 'tp')), may hold values from -6 to 6
- positions: int32 [64], replicated, may hold values from 0 to 511
- w_enc: bfloat16 [8192, 32768], P(None, ('tp', 'lat')), may hold values from -0.0625 to 0.0625
- b_enc: float32 [32768], P(('tp', 'lat')), may hold values from -3 to 3
- dec_norm: float32 [32768], P(('tp', 'lat')), may hold values from 0.05 to 0.5
- b_dec: float32 [8192], replicated, may hold values from -3 to 3
Outputs:
- stream: bfloat16 [512, 8192], P(('lat', 'tp'))
- codes: bfloat16 [64, 32768], P(None, ('tp', 'lat'))
- recon: bfloat16 [64, 8192], P(('tp', 'lat'))
- error: float32 [64], P(('tp', 'lat'))
The draws below stay inside these ranges and needn't reach their ends.
All inputs are finite; a program needn't handle non-finite values.
Results may differ from the reference program's by a relative error of at most 0.0059.
Values may be sent and summed in bfloat16 or wider, within the bound.
A program may use at most 128 MiB of HBM per device.

```python
import math
import jax
import jax.numpy as jnp
from jax import lax

D = 8192
HD = 128
HEADS = 16
LATENTS = 32768
TOKENS = 512
SEL = 64


def set_ends(values, stream_key, smallest, largest):
    longest = values.shape.index(max(values.shape))
    spots = []
    for shift in (0, 1):
        where = [jax.random.randint(jax.random.fold_in(stream_key, axis), (), 0, length) for axis, length in enumerate(values.shape)]
        where[longest] = (where[longest] + shift) % values.shape[longest]
        spots.append(tuple(where))
    return values.at[spots[0]].set(smallest).at[spots[1]].set(largest)


def levels(own_key, extent, cuts, smallest, largest):
    def one(axis_at, blocks):
        draws = jax.random.uniform(jax.random.fold_in(jax.random.fold_in(own_key, 6), axis_at), (blocks,), jnp.float32, smallest / len(cuts), largest / len(cuts))
        return jnp.repeat(jnp.exp(draws), extent[axis_at] // blocks).reshape((-1,) + (1,) * (len(extent) - axis_at - 1))

    loudness = one(*cuts[0])
    for cut in cuts[1:]:
        loudness = loudness * one(*cut)
    return loudness


def scatter_about(stream_key, dims, width, reach, pieces=(), dtype=jnp.bfloat16):
    drawn = width * jax.random.normal(stream_key, dims, jnp.float32)
    if pieces:
        drawn = drawn * levels(stream_key, dims, pieces, -0.22, 0.18)
    return jnp.clip(drawn, -reach, reach).astype(dtype)


def setup_inputs(seed: int = 0) -> dict:
    streams_of = jax.random.split(jax.random.key(seed), 9)
    attn_out = scatter_about(streams_of[0], (TOKENS, HEADS * HD), 1.0, 6.0, ((0, 8), (1, 4)))
    w_out = scatter_about(streams_of[1], (HEADS * HD, D), (HEADS * HD) ** -0.5, 0.125, ((0, 4),))
    resid_in = scatter_about(streams_of[2], (TOKENS, D), 1.0, 6.0, ((0, 32),))
    positions = set_ends(jax.random.randint(streams_of[3], (SEL,), 0, TOKENS), jax.random.fold_in(streams_of[3], 1), 0, TOKENS - 1).astype(jnp.int32)
    w_enc = scatter_about(streams_of[4], (D, LATENTS), D ** -0.5, 0.0625, ((1, 32),))
    b_enc = scatter_about(streams_of[5], (LATENTS,), 0.5, 3.0, ((0, 32),), jnp.float32)
    dec_norm = jnp.clip(jnp.exp(math.log(0.5) - 2.3025851 * jax.random.uniform(streams_of[6], (LATENTS,), jnp.float32) ** levels(streams_of[6], (LATENTS,), ((0, 32),), -0.2, 0.2)), 0.05, 0.5)
    b_dec = scatter_about(streams_of[7], (D,), 0.5, 3.0, (), jnp.float32)
    return dict(attn_out=attn_out, w_out=w_out, resid_in=resid_in, positions=positions, w_enc=w_enc, b_enc=b_enc, dec_norm=dec_norm, b_dec=b_dec)


def reference(attn_out, w_out, resid_in, positions, w_enc, b_enc, dec_norm, b_dec):
    mixed = jnp.dot(attn_out, w_out, preferred_element_type=jnp.float32)
    stream = (resid_in.astype(jnp.float32) + mixed).astype(jnp.bfloat16)
    picked = jnp.take(stream, positions.astype(jnp.int32), axis=0)
    centered = (picked.astype(jnp.float32) - b_dec).astype(jnp.bfloat16)
    pre = jnp.dot(centered, w_enc, preferred_element_type=jnp.float32) + b_enc
    codes = (jnp.maximum(pre, 0.0) * dec_norm).astype(jnp.bfloat16)
    full = lax.dot_general(codes, w_enc, (((1,), (1,)), ((), ())), preferred_element_type=jnp.float32) + b_dec
    recon = full.astype(jnp.bfloat16)
    error = jnp.mean((full - picked.astype(jnp.float32)) ** 2, axis=1)
    return stream, codes, recon, error
```

```python
import functools

import jax
import jax.numpy as jnp
from jax import lax
from jax.experimental import pallas as pl
from jax.experimental.pallas import tpu as pltpu
from jax.sharding import PartitionSpec as P

GROUPS = 4
LANES = 128
F32 = jnp.float32
BF16 = jnp.bfloat16
MESH = pl.DeviceIdType.MESH


def log2(n):
    return n.bit_length() - 1


def orders(n_tp, n_lat):
    tp_bits = [("tp", b) for b in range(log2(n_tp))]
    lat_bits = [("lat", b) for b in range(log2(n_lat))]
    out = []
    for g in range(GROUPS):
        turn = g % max(len(tp_bits), 1)
        out.append(lat_bits[:1] + tp_bits[turn:] + tp_bits[:turn] + lat_bits[1:])
    return out


def kernel(n_tp, n_lat, pos_ref, attn_ref, resid_ref, b_enc_ref, norm_ref, bdec_ref, w_out_hbm, w_enc_hbm,
           stream_ref, codes_ref, recon_ref, err_ref,
           w_out, w_enc, lhs, pick_own, acc, pk, snd, rcv_a, rcv_c, mix_snd, mix_rcv, mix_own, pre, cperm, mine,
           in_sem, enc_sem, a_send, a_recv, g_send, g_recv, c_send, c_recv, m_send, m_recv):
    ids = {"tp": lax.axis_index("tp"), "lat": lax.axis_index("lat")}
    n_dev = n_tp * n_lat
    rows, depth = attn_ref.shape
    own_rows, width = resid_ref.shape
    sel = pos_ref.shape[1]
    cg = width // LANES // GROUPS
    rg = cg * sel
    order = orders(n_tp, n_lat)
    n_steps = len(order[0])
    bit = lambda ab: lax.rem(lax.div(ids[ab[0]], 1 << ab[1]), 2)
    flip = lambda ab: {ab[0]: ids[ab[0]] + (1 - 2 * bit(ab)) * (1 << ab[1])}
    core = bit(order[0][0])
    half_cols = cg * LANES // 2

    def piece(g, which):
        h = 1 - core if which == 0 else core
        return pl.multiple_of(g * cg * LANES + h * half_cols, half_cols)

    loads = []
    for which in range(2):
        for g in range(GROUPS):
            cols = pl.ds(piece(g, which), half_cols)
            loads.append(pltpu.make_async_copy(w_out_hbm.at[:, cols], w_out.at[:, cols], in_sem.at[which * GROUPS + g]))
    n_enc = enc_sem.shape[0]
    enc_rows = width // n_enc
    enc_loads = [
        pltpu.make_async_copy(w_enc_hbm.at[pl.ds(i * enc_rows, enc_rows), :], w_enc.at[pl.ds(i * enc_rows, enc_rows), :], enc_sem.at[i])
        for i in range(n_enc)
    ]
    for load in loads + enc_loads:
        load.start()

    barrier = pltpu.get_barrier_semaphore()
    peers = [flip(("lat", b)) for b in range(log2(n_lat))]
    mix_peer = lambda d: lax.rem(ids["tp"] + d, n_tp)
    peers += [{"tp": mix_peer(d)} for d in range(1, n_tp)]
    for peer in peers:
        pl.semaphore_signal(barrier, inc=1, device_id=peer, device_id_type=MESH)

    base = ids["lat"] * rows
    hot = (lax.broadcasted_iota(jnp.int32, (rows, sel), 0) + base == pos_ref[...]).astype(BF16)
    lhs[0:rows, :] = attn_ref[...]
    lhs[rows:rows + sel, :] = lax.dot_general(hot, attn_ref[...], (((0,), (0,)), ((), ())), preferred_element_type=F32).astype(BF16)
    lhs[rows + sel:rows + sel + own_rows, :] = attn_ref[pl.ds(pl.multiple_of(ids["tp"] * own_rows, own_rows), own_rows), :]
    base = (ids["lat"] * n_tp + ids["tp"]) * own_rows
    hot = (lax.broadcasted_iota(jnp.int32, (own_rows, sel), 0) + base == pos_ref[...]).astype(BF16)
    eye = (lax.broadcasted_iota(jnp.int32, (own_rows, own_rows), 0) == lax.broadcasted_iota(jnp.int32, (own_rows, own_rows), 1)).astype(BF16)
    pick_own[...] = lax.dot_general(hot, eye, (((0,), (0,)), ((), ())), preferred_element_type=F32).astype(BF16)

    def halves(s):
        return rg - (rg >> s), rg >> (s + 1)

    def exchange(rcv, send_sem, recv_sem, g, s):
        off, size = halves(s)
        return pltpu.make_async_remote_copy(
            src_ref=snd.at[g, pl.ds(off, size), :],
            dst_ref=rcv.at[g, pl.ds(off, size), :],
            send_sem=send_sem.at[g * n_steps + s],
            recv_sem=recv_sem.at[g * n_steps + s],
            device_id=flip(order[g][s]),
            device_id_type=MESH,
        )

    tile = min(512, half_cols)
    per = tile // LANES
    for which in range(2):
        for g in range(GROUPS):
            loads[which * GROUPS + g].wait()
            first = piece(g, which)

            def body(i, _, which=which, g=g, first=first):
                cols = pl.ds(pl.multiple_of(first + i * tile, tile), tile)
                out = jnp.dot(lhs[...], w_out[:, cols], preferred_element_type=F32)
                mix_snd[:, cols] = out[0:rows].astype(BF16)
                mix_own[:, cols] = out[rows + sel:]
                part = out[rows:rows + sel] + jnp.dot(pick_own[...], resid_ref[:, cols], preferred_element_type=F32)
                for k in range(per):
                    block = part[:, k * LANES:(k + 1) * LANES]
                    at = (i * per + k) * sel
                    if which == 0:
                        snd[g, pl.ds(pl.multiple_of(at, sel), sel), :] = block.astype(BF16)
                    else:
                        acc[pl.ds(pl.multiple_of(g * rg + core * (rg // 2) + at, sel), sel), :] = block
                return 0

            lax.fori_loop(0, half_cols // tile, body, 0)
            if which == 0:
                if g == 0:
                    pl.semaphore_wait(barrier, len(peers))
                exchange(rcv_a, a_send, a_recv, g, 0).start()

    def starts(g):
        out = [0]
        for s in range(n_steps):
            out.append(out[-1] + bit(order[g][s]) * (rg >> (s + 1)))
        return out

    start = [starts(g) for g in range(GROUPS)]

    def span(at, size):
        return pl.ds(pl.multiple_of(at, size), size)

    def reduce(rcv, send_sem, recv_sem, last, between=None):
        for s in range(n_steps):
            off, size = halves(s)
            for g in range(GROUPS):
                exchange(rcv, send_sem, recv_sem, g, s).wait_recv()
                here = start[g][s + 1]
                if s + 1 < n_steps:
                    half = size // 2
                    b = bit(order[g][s + 1])
                    gone, kept = (1 - b) * half, b * half
                    to = halves(s + 1)[0]
                    snd[g, pl.ds(to, half), :] = (
                        acc[span(g * rg + here + gone, half), :] + rcv[g, span(off + gone, half), :].astype(F32)
                    ).astype(BF16)
                    exchange(rcv, send_sem, recv_sem, g, s + 1).start()
                    at = span(g * rg + here + kept, half)
                    acc[at, :] = acc[at, :] + rcv[g, span(off + kept, half), :].astype(F32)
                else:
                    last(g, here, size, acc[span(g * rg + here, size), :] + rcv[g, pl.ds(off, size), :].astype(F32))
            if s == 0 and between is not None:
                between()
        for s in range(n_steps):
            for g in range(GROUPS):
                exchange(rcv, send_sem, recv_sem, g, s).wait_send()

    def own_rows_done(g, here, size, total):
        pk[span(g * rg + here, size), :] = total.astype(BF16)

    reduce(rcv_a, a_send, a_recv, own_rows_done)

    def share(g, s):
        at = span(g * rg + start[g][s + 1], rg >> (s + 1))
        return pltpu.make_async_remote_copy(
            src_ref=pk.at[at, :],
            dst_ref=pk.at[at, :],
            send_sem=g_send.at[g * n_steps + s],
            recv_sem=g_recv.at[g * n_steps + s],
            device_id=flip(order[g][s]),
            device_id_type=MESH,
        )

    pre[...] = jnp.zeros_like(pre)
    n_tile = min(256, pre.shape[1])

    def encode(g, at, size):
        count = size // sel
        first = g * cg + lax.div(at, sel)
        parts = []
        for k in range(count):
            ct = first + k
            block = pk[pl.ds(pl.multiple_of(ct * sel, sel), sel), :].astype(F32)
            acc[pl.ds(pl.multiple_of(ct * sel, sel), sel), :] = block
            parts.append((block - bdec_ref[pl.ds(ct, 1), :]).astype(BF16))
        left = jnp.concatenate(parts, axis=1)
        deep = pl.ds(pl.multiple_of(first * LANES, count * LANES), count * LANES)

        def body(i, _):
            cols = pl.ds(pl.multiple_of(i * n_tile, n_tile), n_tile)
            pre[:, cols] += jnp.dot(left, w_enc[deep, cols], preferred_element_type=F32)
            return 0

        lax.fori_loop(0, pre.shape[1] // n_tile, body, 0)

    for s in reversed(range(n_steps)):
        for g in range(GROUPS):
            share(g, s).start()
        if s == 1:
            for load in enc_loads:
                load.wait()
        if s <= 1:
            for g in range(GROUPS):
                size = rg >> (s + 1)
                if s == 1:
                    encode(g, start[g][2], size)
                else:
                    encode(g, start[g][1] + (1 - bit(order[g][1])) * (rg >> 2), rg >> 2)
        for g in range(GROUPS):
            share(g, s).wait_recv()

    def mix(d):
        to = mix_peer(d)
        return pltpu.make_async_remote_copy(
            src_ref=mix_snd.at[pl.ds(pl.multiple_of(to * own_rows, own_rows), own_rows), :],
            dst_ref=mix_rcv.at[d - 1],
            send_sem=m_send.at[d - 1],
            recv_sem=m_recv.at[d - 1],
            device_id={"tp": to},
            device_id_type=MESH,
        )

    for d in range(1, n_tp):
        mix(d).start()
    for g in range(GROUPS):
        encode(g, (1 - core) * (rg // 2), rg // 2)
    for s in range(n_steps):
        for g in range(GROUPS):
            share(g, s).wait_send()

    codes = (jnp.maximum(pre[...] + b_enc_ref[...], 0.0) * norm_ref[...]).astype(BF16)
    codes_ref[...] = codes

    keep = sel // n_dev
    me = ids["tp"] * n_lat + ids["lat"]
    for r in range(keep):
        mine[r] = acc[pl.ds(me * keep + r, width // LANES, stride=sel), :]

    kinds = {}
    for g in range(GROUPS):
        if tuple(order[g]) not in kinds:
            q = lax.broadcasted_iota(jnp.int32, (sel, sel), 0)
            chunk = lax.div(q, keep)
            row = lax.rem(q, keep)
            for i, (axis, b) in enumerate(order[g]):
                weight = keep * (1 << b) * (n_lat if axis == "tp" else 1)
                row = row + lax.rem(lax.div(chunk, 1 << (n_steps - 1 - i)), 2) * weight
            turn = (row == lax.broadcasted_iota(jnp.int32, (sel, sel), 1)).astype(BF16)
            kinds[tuple(order[g])] = len(kinds)
            cperm[len(kinds) - 1] = jnp.dot(turn, codes, preferred_element_type=F32).astype(BF16)
    d_tile = min(256, cg * LANES)
    d_per = d_tile // LANES
    for g in range(GROUPS):
        left = cperm[kinds[tuple(order[g])]]

        def body(i, _, g=g, left=left):
            at = pl.ds(pl.multiple_of(g * cg * LANES + i * d_tile, d_tile), d_tile)
            out = lax.dot_general(left, w_enc[at, :], (((1,), (1,)), ((), ())), preferred_element_type=F32)
            for k in range(d_per):
                acc[pl.ds(g * rg + i * d_per + k, sel, stride=cg), :] = out[:, k * LANES:(k + 1) * LANES]
            return 0

        lax.fori_loop(0, cg * LANES // d_tile, body, 0)
        half = rg // 2
        snd[g, pl.ds(0, half), :] = acc[span(g * rg + (1 - core) * half, half), :].astype(BF16)
        exchange(rcv_c, c_send, c_recv, g, 0).start()

    sums = [None] * keep

    def score(g, here, size, total):
        for r in range(keep):
            full = total[r * cg:(r + 1) * cg] + bdec_ref[g * cg:(g + 1) * cg, :]
            recon_ref[r * (width // LANES) + g * cg:r * (width // LANES) + (g + 1) * cg, :] = full.astype(BF16)
            off = full - mine[r, g * cg:(g + 1) * cg, :]
            sums[r] = off * off if sums[r] is None else sums[r] + off * off

    def keep_stream():
        for d in range(1, n_tp):
            mix(d).wait_recv()

        def body(i, _):
            cols = pl.ds(pl.multiple_of(i * 1024, 1024), 1024)
            total = mix_own[:, cols]
            for d in range(1, n_tp):
                total = total + mix_rcv[d - 1, :, cols].astype(F32)
            stream_ref[:, cols] = (resid_ref[:, cols].astype(F32) + total).astype(BF16)
            return 0

        lax.fori_loop(0, width // 1024, body, 0)

    reduce(rcv_c, c_send, c_recv, score, keep_stream)
    for r in range(keep):
        total = jnp.sum(jnp.sum(sums[r], axis=0, keepdims=True), axis=1, keepdims=True) / width
        err_ref[r:r + 1, :] = jnp.broadcast_to(total, (1, LANES))
    for d in range(1, n_tp):
        mix(d).wait_send()


def shards(attn_out, w_out, resid_in, positions, w_enc, b_enc, dec_norm, b_dec):
    n_tp = lax.axis_size("tp")
    n_lat = lax.axis_size("lat")
    n_dev = n_tp * n_lat
    rows, depth = attn_out.shape
    own_rows, width = resid_in.shape
    sel = positions.shape[0]
    lats = w_enc.shape[1]
    keep = sel // n_dev
    feats = width // LANES
    rg = feats // GROUPS * sel
    n_steps = log2(n_dev)
    vmem = pl.BlockSpec(memory_space=pltpu.VMEM)
    hbm = pl.BlockSpec(memory_space=pl.ANY)
    dma = pltpu.SemaphoreType.DMA
    n_sem = GROUPS * n_steps
    stream, codes, recon, err = pl.pallas_call(
        functools.partial(kernel, n_tp, n_lat),
        out_shape=(
            jax.ShapeDtypeStruct((own_rows, width), BF16),
            jax.ShapeDtypeStruct((sel, lats), BF16),
            jax.ShapeDtypeStruct((keep * feats, LANES), BF16),
            jax.ShapeDtypeStruct((keep, LANES), F32),
        ),
        in_specs=[vmem] * 6 + [hbm] * 2,
        out_specs=(vmem,) * 4,
        scratch_shapes=[
            pltpu.VMEM((depth, width), BF16),
            pltpu.VMEM((width, lats), BF16),
            pltpu.VMEM((rows + sel + own_rows, depth), BF16),
            pltpu.VMEM((sel, own_rows), BF16),
            pltpu.VMEM((GROUPS * rg, LANES), F32),
            pltpu.VMEM((GROUPS * rg, LANES), BF16),
            pltpu.VMEM((GROUPS, rg, LANES), BF16),
            pltpu.VMEM((GROUPS, rg, LANES), BF16),
            pltpu.VMEM((GROUPS, rg, LANES), BF16),
            pltpu.VMEM((rows, width), BF16),
            pltpu.VMEM((n_tp - 1, own_rows, width), BF16),
            pltpu.VMEM((own_rows, width), F32),
            pltpu.VMEM((sel, lats), F32),
            pltpu.VMEM((min(GROUPS, log2(n_tp)), sel, lats), BF16),
            pltpu.VMEM((keep, feats, LANES), F32),
            dma((2 * GROUPS,)),
            dma((8,)),
            dma((n_sem,)), dma((n_sem,)),
            dma((n_sem,)), dma((n_sem,)),
            dma((n_sem,)), dma((n_sem,)),
            dma((n_tp - 1,)), dma((n_tp - 1,)),
        ],
        compiler_params=pltpu.CompilerParams(
            collective_id=0, has_side_effects=True, vmem_limit_bytes=60 * 1024 * 1024
        ),
        cost_estimate=pl.CostEstimate(
            flops=2 * (2 * sel * width * lats + (rows + sel + own_rows) * depth * width),
            bytes_accessed=2 * (w_out.size + w_enc.size),
            transcendentals=0,
        ),
    )(
        positions.reshape(1, sel),
        attn_out,
        resid_in,
        b_enc.reshape(1, lats),
        dec_norm.reshape(1, lats),
        b_dec.reshape(feats, LANES),
        w_out,
        w_enc,
    )
    return stream, codes, recon.reshape(keep, width), err[:, 0]


def solution(mesh):
    placed = (
        P("lat", "tp"),
        P("tp", None),
        P(("lat", "tp"), None),
        P(),
        P(None, ("tp", "lat")),
        P(("tp", "lat")),
        P(("tp", "lat")),
        P(),
    )
    return jax.shard_map(
        shards,
        mesh=mesh,
        in_specs=placed,
        out_specs=(
            P(("lat", "tp"), None),
            P(None, ("tp", "lat")),
            P(("tp", "lat"), None),
            P(("tp", "lat")),
        ),
        check_vma=False,
    )
```

```python
import functools

import jax
import jax.numpy as jnp
from jax import lax
from jax.experimental import pallas as pl
from jax.experimental.pallas import tpu as pltpu
from jax.sharding import PartitionSpec as P

GROUPS = 4
LANES = 128
F32 = jnp.float32
BF16 = jnp.bfloat16
MESH = pl.DeviceIdType.MESH


def log2(n):
    return n.bit_length() - 1


def digits(n_tp, n_lat):
    tp_bits, lat_bits = log2(n_tp), log2(n_lat)
    out = [("lat", 0, 2)] if lat_bits else []
    out += [("tp", b, 1 << min(2, tp_bits - b)) for b in range(0, tp_bits, 2)]
    out += [("lat", b, 1 << min(2, lat_bits - b)) for b in range(1, lat_bits, 2)]
    return out


def kernel(n_tp, n_lat, pos_ref, attn_ref, resid_ref, b_enc_ref, norm_ref, bdec_ref, w_out_hbm, w_enc_hbm,
           stream_ref, codes_ref, recon_ref, err_ref,
           w_out, w_enc, lhs, pick_own, acc, pk, snd, rcv_a, rcv_c, mix_snd, mix_rcv, mix_own, pre, cperm, mine,
           in_sem, enc_sem, a_send, a_recv, g_send, g_recv, c_send, c_recv, m_send, m_recv):
    ids = {"tp": lax.axis_index("tp"), "lat": lax.axis_index("lat")}
    n_dev = n_tp * n_lat
    rows, depth = attn_ref.shape
    own_rows, width = resid_ref.shape
    sel = pos_ref.shape[1]
    cg = width // LANES // GROUPS
    rg = cg * sel
    steps = digits(n_tp, n_lat)
    n_steps = len(steps)
    digit = [lax.rem(lax.div(ids[axis], 1 << low), radix) for axis, low, radix in steps]
    sizes = [rg]
    for axis, low, radix in steps:
        sizes.append(sizes[-1] // radix)
    offs = [0]
    sem_at = [0]
    for s in range(n_steps):
        offs.append(offs[-1] + (steps[s][2] - 1) * sizes[s + 1])
        sem_at.append(sem_at[-1] + steps[s][2] - 1)
    start = [0]
    for s in range(n_steps):
        start.append(start[-1] + digit[s] * sizes[s + 1])

    def towards(s, d):
        return lax.rem(digit[s] + d, steps[s][2])

    def peer(s, d):
        axis, low, radix = steps[s]
        return {axis: ids[axis] + (towards(s, d) - digit[s]) * (1 << low)}

    core = digit[0]
    half_cols = cg * LANES // 2

    def piece(g, which):
        h = 1 - core if which == 0 else core
        return pl.multiple_of(g * cg * LANES + h * half_cols, half_cols)

    def load(g, which):
        cols = pl.ds(piece(g, which), half_cols)
        return pltpu.make_async_copy(w_out_hbm.at[:, cols], w_out.at[:, cols], in_sem.at[which * GROUPS + g])

    load(0, 0).start()
    for g in range(GROUPS):
        if g + 1 < GROUPS:
            load(g + 1, 0).start()
        load(g, 1).start()
    n_enc = enc_sem.shape[0]
    enc_rows = width // n_enc
    enc_loads = [
        pltpu.make_async_copy(w_enc_hbm.at[pl.ds(i * enc_rows, enc_rows), :], w_enc.at[pl.ds(i * enc_rows, enc_rows), :], enc_sem.at[i])
        for i in range(n_enc)
    ]
    for one in enc_loads:
        one.start()

    barrier = pltpu.get_barrier_semaphore()
    mix_peer = lambda d: lax.rem(ids["tp"] + d, n_tp)
    peers = [peer(s, d) for s in range(n_steps) if steps[s][0] == "lat" for d in range(1, steps[s][2])]
    peers += [{"tp": mix_peer(d)} for d in range(1, n_tp)]
    for one in peers:
        pl.semaphore_signal(barrier, inc=1, device_id=one, device_id_type=MESH)

    base = ids["lat"] * rows
    hot = (lax.broadcasted_iota(jnp.int32, (rows, sel), 0) + base == pos_ref[...]).astype(BF16)
    lhs[0:rows, :] = attn_ref[...]
    lhs[rows:rows + sel, :] = lax.dot_general(hot, attn_ref[...], (((0,), (0,)), ((), ())), preferred_element_type=F32).astype(BF16)
    lhs[rows + sel:rows + sel + own_rows, :] = attn_ref[pl.ds(pl.multiple_of(ids["tp"] * own_rows, own_rows), own_rows), :]
    base = (ids["lat"] * n_tp + ids["tp"]) * own_rows
    hot = (lax.broadcasted_iota(jnp.int32, (own_rows, sel), 0) + base == pos_ref[...]).astype(BF16)
    eye = (lax.broadcasted_iota(jnp.int32, (own_rows, own_rows), 0) == lax.broadcasted_iota(jnp.int32, (own_rows, own_rows), 1)).astype(BF16)
    pick_own[...] = lax.dot_general(hot, eye, (((0,), (0,)), ((), ())), preferred_element_type=F32).astype(BF16)

    def span(at, size):
        return pl.ds(pl.multiple_of(at, size), size)

    def exchange(rcv, send_sem, recv_sem, g, s, d):
        at = pl.ds(offs[s] + (d - 1) * sizes[s + 1], sizes[s + 1])
        sem = g * sem_at[-1] + sem_at[s] + d - 1
        return pltpu.make_async_remote_copy(
            src_ref=snd.at[g, at, :],
            dst_ref=rcv.at[g, at, :],
            send_sem=send_sem.at[sem],
            recv_sem=recv_sem.at[sem],
            device_id=peer(s, d),
            device_id_type=MESH,
        )

    tile = min(512, half_cols)
    per = tile // LANES

    def project(g, which):
        load(g, which).wait()
        first = piece(g, which)

        def body(i, _):
            cols = pl.ds(pl.multiple_of(first + i * tile, tile), tile)
            out = jnp.dot(lhs[...], w_out[:, cols], preferred_element_type=F32)
            mix_snd[:, cols] = out[0:rows].astype(BF16)
            mix_own[:, cols] = out[rows + sel:]
            part = out[rows:rows + sel] + jnp.dot(pick_own[...], resid_ref[:, cols], preferred_element_type=F32)
            for k in range(per):
                block = part[:, k * LANES:(k + 1) * LANES]
                at = (i * per + k) * sel
                if which == 0:
                    snd[g, pl.ds(pl.multiple_of(at, sel), sel), :] = block.astype(BF16)
                else:
                    acc[pl.ds(pl.multiple_of(g * rg + core * (rg // 2) + at, sel), sel), :] = block
            return 0

        lax.fori_loop(0, half_cols // tile, body, 0)
        if which == 0:
            if g == 0:
                pl.semaphore_wait(barrier, len(peers))
            exchange(rcv_a, a_send, a_recv, g, 0, 1).start()

    def take(rcv, send_sem, recv_sem, last, g, s):
        radix = steps[s][2]
        for d in range(1, radix):
            exchange(rcv, send_sem, recv_sem, g, s, d).wait_recv()

        def total(at, size):
            out = acc[span(g * rg + start[s + 1] + at, size), :]
            for d in range(1, radix):
                out = out + rcv[g, span(offs[s] + (d - 1) * sizes[s + 1] + at, size), :].astype(F32)
            return out

        if s + 1 == n_steps:
            last(g, total(0, sizes[s + 1]))
            return
        size = sizes[s + 2]
        for d in range(1, steps[s + 1][2]):
            snd[g, pl.ds(offs[s + 1] + (d - 1) * size, size), :] = total(towards(s + 1, d) * size, size).astype(BF16)
            exchange(rcv, send_sem, recv_sem, g, s + 1, d).start()
        acc[span(g * rg + start[s + 2], size), :] = total(digit[s + 1] * size, size)

    def sent(rcv, send_sem, recv_sem):
        for g in range(GROUPS):
            for s in range(n_steps):
                for d in range(1, steps[s][2]):
                    exchange(rcv, send_sem, recv_sem, g, s, d).wait_send()

    def share(g, s, d):
        at = span(g * rg + start[s + 1], sizes[s + 1])
        sem = g * sem_at[-1] + sem_at[s] + d - 1
        return pltpu.make_async_remote_copy(
            src_ref=pk.at[at, :],
            dst_ref=pk.at[at, :],
            send_sem=g_send.at[sem],
            recv_sem=g_recv.at[sem],
            device_id=peer(s, d),
            device_id_type=MESH,
        )

    def share_start(g, s):
        for d in range(1, steps[s][2]):
            share(g, s, d).start()

    def share_take(g, s):
        for d in range(1, steps[s][2]):
            share(g, s, d).wait_recv()

    def own_rows_done(g, total):
        pk[span(g * rg + start[n_steps], sizes[n_steps]), :] = total.astype(BF16)
        share_start(g, n_steps - 1)

    n_tile = min(256, pre.shape[1])

    def encode(g, at, size):
        count = size // sel
        first = g * cg + lax.div(at, sel)
        parts = []
        for k in range(count):
            ct = first + k
            block = pk[pl.ds(pl.multiple_of(ct * sel, sel), sel), :].astype(F32)
            acc[pl.ds(pl.multiple_of(ct * sel, sel), sel), :] = block
            parts.append((block - bdec_ref[pl.ds(ct, 1), :]).astype(BF16))
        left = jnp.concatenate(parts, axis=1)
        deep = pl.ds(pl.multiple_of(first * LANES, count * LANES), count * LANES)

        def body(i, _):
            cols = pl.ds(pl.multiple_of(i * n_tile, n_tile), n_tile)
            pre[:, cols] += jnp.dot(left, w_enc[deep, cols], preferred_element_type=F32)
            return 0

        lax.fori_loop(0, pre.shape[1] // n_tile, body, 0)

    def mix(d):
        to = mix_peer(d)
        return pltpu.make_async_remote_copy(
            src_ref=mix_snd.at[pl.ds(pl.multiple_of(to * own_rows, own_rows), own_rows), :],
            dst_ref=mix_rcv.at[d - 1],
            send_sem=m_send.at[d - 1],
            recv_sem=m_recv.at[d - 1],
            device_id={"tp": to},
            device_id_type=MESH,
        )

    def wave(ops, after=None):
        for t in range(len(ops) + GROUPS - 1):
            for g in reversed(range(GROUPS)):
                if 0 <= t - g < len(ops):
                    ops[t - g](g)
            if after is not None:
                after(t)

    def encode_near(g):
        share_take(g, 1)
        share_start(g, 0)
        if g == GROUPS - 1:
            for d in range(1, n_tp):
                mix(d).start()
        if g == 0:
            for one in enc_loads:
                one.wait()
        encode(g, start[1], rg // 2)

    def encode_far(g):
        share_take(g, 0)
        encode(g, (1 - core) * (rg // 2), rg // 2)

    def pass_on(g, s):
        share_take(g, s)
        share_start(g, s - 1)

    pre[...] = jnp.zeros_like(pre)
    ops = [functools.partial(project, which=0), functools.partial(project, which=1)]
    ops += [functools.partial(take, rcv_a, a_send, a_recv, own_rows_done, s=s) for s in range(n_steps)]
    ops += [functools.partial(pass_on, s=s) for s in reversed(range(2, n_steps))]
    ops += [encode_near, encode_far]
    wave(ops)
    sent(rcv_a, a_send, a_recv)
    for g in range(GROUPS):
        for s in range(n_steps):
            for d in range(1, steps[s][2]):
                share(g, s, d).wait_send()

    codes = (jnp.maximum(pre[...] + b_enc_ref[...], 0.0) * norm_ref[...]).astype(BF16)
    codes_ref[...] = codes

    keep = sel // n_dev
    me = ids["tp"] * n_lat + ids["lat"]
    for r in range(keep):
        mine[r] = acc[pl.ds(me * keep + r, width // LANES, stride=sel), :]

    q = lax.broadcasted_iota(jnp.int32, (sel, sel), 0)
    row = lax.rem(q, keep)
    for s, (axis, low, radix) in enumerate(steps):
        weight = keep * (1 << low) * (n_lat if axis == "tp" else 1)
        row = row + lax.rem(lax.div(q, sizes[s + 1] // cg), radix) * weight
    turn = (row == lax.broadcasted_iota(jnp.int32, (sel, sel), 1)).astype(BF16)
    cperm[...] = jnp.dot(turn, codes, preferred_element_type=F32).astype(BF16)
    d_tile = min(256, cg * LANES)
    d_per = d_tile // LANES

    def decode(g):
        left = cperm[...]

        def body(i, _):
            at = pl.ds(pl.multiple_of(g * cg * LANES + i * d_tile, d_tile), d_tile)
            out = lax.dot_general(left, w_enc[at, :], (((1,), (1,)), ((), ())), preferred_element_type=F32)
            for k in range(d_per):
                acc[pl.ds(g * rg + i * d_per + k, sel, stride=cg), :] = out[:, k * LANES:(k + 1) * LANES]
            return 0

        lax.fori_loop(0, cg * LANES // d_tile, body, 0)
        half = rg // 2
        snd[g, pl.ds(0, half), :] = acc[span(g * rg + (1 - core) * half, half), :].astype(BF16)
        exchange(rcv_c, c_send, c_recv, g, 0, 1).start()

    sums = [None] * keep

    def score(g, total):
        for r in range(keep):
            full = total[r * cg:(r + 1) * cg] + bdec_ref[g * cg:(g + 1) * cg, :]
            recon_ref[r * (width // LANES) + g * cg:r * (width // LANES) + (g + 1) * cg, :] = full
            off = full - mine[r, g * cg:(g + 1) * cg, :]
            sums[r] = off * off if sums[r] is None else sums[r] + off * off

    def keep_stream(t):
        if t != GROUPS:
            return
        for d in range(1, n_tp):
            mix(d).wait_recv()

        def body(i, _):
            cols = pl.ds(pl.multiple_of(i * 1024, 1024), 1024)
            total = mix_own[:, cols]
            for d in range(1, n_tp):
                total = total + mix_rcv[d - 1, :, cols].astype(F32)
            stream_ref[:, cols] = (resid_ref[:, cols].astype(F32) + total).astype(BF16)
            return 0

        lax.fori_loop(0, width // 1024, body, 0)

    ops = [decode] + [functools.partial(take, rcv_c, c_send, c_recv, score, s=s) for s in range(n_steps)]
    wave(ops, keep_stream)
    for r in range(keep):
        total = jnp.sum(jnp.sum(sums[r], axis=0, keepdims=True), axis=1, keepdims=True) / width
        err_ref[r:r + 1, :] = jnp.broadcast_to(total, (1, LANES))
    sent(rcv_c, c_send, c_recv)
    for d in range(1, n_tp):
        mix(d).wait_send()


def finish(stream_in, codes_in, recon_in, err_in, stream_ref, codes_ref, recon_ref, err_ref):
    stream_ref[...] = stream_in[...]
    codes_ref[...] = codes_in[...]
    keep, width = recon_ref.shape
    feats = width // LANES
    for c in range(feats):
        recon_ref[:, c * LANES:(c + 1) * LANES] = recon_in[pl.ds(c, keep, stride=feats), :].astype(BF16)
    for r in range(keep):
        err_ref[r] = err_in[r, 0]


def shards(attn_out, w_out, resid_in, positions, w_enc, b_enc, dec_norm, b_dec):
    n_tp = lax.axis_size("tp")
    n_lat = lax.axis_size("lat")
    n_dev = n_tp * n_lat
    rows, depth = attn_out.shape
    own_rows, width = resid_in.shape
    sel = positions.shape[0]
    lats = w_enc.shape[1]
    keep = sel // n_dev
    feats = width // LANES
    rg = feats // GROUPS * sel
    n_sem = GROUPS * sum(radix - 1 for _, _, radix in digits(n_tp, n_lat))
    vmem = pl.BlockSpec(memory_space=pltpu.VMEM)
    hbm = pl.BlockSpec(memory_space=pl.ANY)
    dma = pltpu.SemaphoreType.DMA
    made = pl.pallas_call(
        functools.partial(kernel, n_tp, n_lat),
        out_shape=(
            jax.ShapeDtypeStruct((own_rows, width), BF16),
            jax.ShapeDtypeStruct((sel, lats), BF16),
            jax.ShapeDtypeStruct((keep * feats, LANES), F32),
            jax.ShapeDtypeStruct((keep, LANES), F32),
        ),
        in_specs=[vmem] * 6 + [hbm] * 2,
        out_specs=(vmem,) * 4,
        scratch_shapes=[
            pltpu.VMEM((depth, width), BF16),
            pltpu.VMEM((width, lats), BF16),
            pltpu.VMEM((rows + sel + own_rows, depth), BF16),
            pltpu.VMEM((sel, own_rows), BF16),
            pltpu.VMEM((GROUPS * rg, LANES), F32),
            pltpu.VMEM((GROUPS * rg, LANES), BF16),
            pltpu.VMEM((GROUPS, rg, LANES), BF16),
            pltpu.VMEM((GROUPS, rg, LANES), BF16),
            pltpu.VMEM((GROUPS, rg, LANES), BF16),
            pltpu.VMEM((rows, width), BF16),
            pltpu.VMEM((n_tp - 1, own_rows, width), BF16),
            pltpu.VMEM((own_rows, width), F32),
            pltpu.VMEM((sel, lats), F32),
            pltpu.VMEM((sel, lats), BF16),
            pltpu.VMEM((keep, feats, LANES), F32),
            dma((2 * GROUPS,)),
            dma((8,)),
            dma((n_sem,)), dma((n_sem,)),
            dma((n_sem,)), dma((n_sem,)),
            dma((n_sem,)), dma((n_sem,)),
            dma((n_tp - 1,)), dma((n_tp - 1,)),
        ],
        compiler_params=pltpu.CompilerParams(
            collective_id=0, has_side_effects=True, vmem_limit_bytes=60 * 1024 * 1024
        ),
        cost_estimate=pl.CostEstimate(
            flops=2 * (2 * sel * width * lats + (rows + sel + own_rows) * depth * width),
            bytes_accessed=2 * (w_out.size + w_enc.size),
            transcendentals=0,
        ),
    )(
        positions.reshape(1, sel),
        attn_out,
        resid_in,
        b_enc.reshape(1, lats),
        dec_norm.reshape(1, lats),
        b_dec.reshape(feats, LANES),
        w_out,
        w_enc,
    )
    smem = pl.BlockSpec(memory_space=pltpu.SMEM)
    return pl.pallas_call(
        finish,
        out_shape=(
            jax.ShapeDtypeStruct((own_rows, width), BF16),
            jax.ShapeDtypeStruct((sel, lats), BF16),
            jax.ShapeDtypeStruct((keep, width), BF16),
            jax.ShapeDtypeStruct((keep,), F32),
        ),
        in_specs=[vmem] * 3 + [smem],
        out_specs=(vmem,) * 3 + (smem,),
    )(*made)


def solution(mesh):
    placed = (
        P("lat", "tp"),
        P("tp", None),
        P(("lat", "tp"), None),
        P(),
        P(None, ("tp", "lat")),
        P(("tp", "lat")),
        P(("tp", "lat")),
        P(),
    )
    return jax.shard_map(
        shards,
        mesh=mesh,
        in_specs=placed,
        out_specs=(
            P(("lat", "tp"), None),
            P(None, ("tp", "lat")),
            P(("tp", "lat"), None),
            P(("tp", "lat")),
        ),
        check_vma=False,
    )
```

```python
import functools

import jax
import jax.numpy as jnp
from jax import lax
from jax.experimental import pallas as pl
from jax.experimental.pallas import tpu as pltpu
from jax.sharding import PartitionSpec as P

GROUPS = 4
LANES = 128
F32 = jnp.float32
BF16 = jnp.bfloat16
MESH = pl.DeviceIdType.MESH


def log2(n):
    return n.bit_length() - 1


def digits(n_tp, n_lat):
    tp_bits, lat_bits = log2(n_tp), log2(n_lat)
    out = [("lat", 0, 2)] if lat_bits else []
    out += [("tp", b, 1 << min(2, tp_bits - b)) for b in range(0, tp_bits, 2)]
    out += [("lat", b, 1 << min(2, lat_bits - b)) for b in range(1, lat_bits, 2)]
    return out


def kernel(n_tp, n_lat, pos_ref, attn_ref, resid_ref, b_enc_ref, norm_ref, bdec_ref, w_out_hbm, w_enc_hbm,
           stream_ref, codes_ref, recon_ref, err_ref,
           w_out, w_enc, lhs, pick_own, acc, pk, snd, rcv_a, rcv_c, mix_snd, mix_rcv, mix_own, pre, cperm, mine,
           in_sem, enc_sem, a_send, a_recv, g_send, g_recv, c_send, c_recv, m_send, m_recv):
    ids = {"tp": lax.axis_index("tp"), "lat": lax.axis_index("lat")}
    n_dev = n_tp * n_lat
    rows, depth = attn_ref.shape
    own_rows, width = resid_ref.shape
    sel = pos_ref.shape[1]
    cg = width // LANES // GROUPS
    rg = cg * sel
    steps = digits(n_tp, n_lat)
    n_steps = len(steps)
    digit = [lax.rem(lax.div(ids[axis], 1 << low), radix) for axis, low, radix in steps]
    sizes = [rg]
    for axis, low, radix in steps:
        sizes.append(sizes[-1] // radix)
    offs = [0]
    sem_at = [0]
    for s in range(n_steps):
        offs.append(offs[-1] + (steps[s][2] - 1) * sizes[s + 1])
        sem_at.append(sem_at[-1] + steps[s][2] - 1)
    start = [0]
    for s in range(n_steps):
        start.append(start[-1] + digit[s] * sizes[s + 1])

    def towards(s, d):
        return lax.rem(digit[s] + d, steps[s][2])

    def peer(s, d):
        axis, low, radix = steps[s]
        return {axis: ids[axis] + (towards(s, d) - digit[s]) * (1 << low)}

    core = digit[0]
    half_cols = cg * LANES // 2

    def piece(g, which):
        h = 1 - core if which == 0 else core
        return pl.multiple_of(g * cg * LANES + h * half_cols, half_cols)

    def load(g, which):
        cols = pl.ds(piece(g, which), half_cols)
        return pltpu.make_async_copy(w_out_hbm.at[:, cols], w_out.at[:, cols], in_sem.at[which * GROUPS + g])

    load(0, 0).start()
    for g in range(GROUPS):
        if g + 1 < GROUPS:
            load(g + 1, 0).start()
        load(g, 1).start()
    n_enc = enc_sem.shape[0]
    enc_rows = width // n_enc
    enc_loads = [
        pltpu.make_async_copy(w_enc_hbm.at[pl.ds(i * enc_rows, enc_rows), :], w_enc.at[pl.ds(i * enc_rows, enc_rows), :], enc_sem.at[i])
        for i in range(n_enc)
    ]

    barrier = pltpu.get_barrier_semaphore()
    mix_peer = lambda d: lax.rem(ids["tp"] + d, n_tp)
    peers = [peer(s, d) for s in range(n_steps) if steps[s][0] == "lat" for d in range(1, steps[s][2])]
    peers += [{"tp": mix_peer(d)} for d in range(1, n_tp)]
    for one in peers:
        pl.semaphore_signal(barrier, inc=1, device_id=one, device_id_type=MESH)

    base = ids["lat"] * rows
    hot = (lax.broadcasted_iota(jnp.int32, (rows, sel), 0) + base == pos_ref[...]).astype(BF16)
    lhs[0:rows, :] = attn_ref[...]
    lhs[rows:rows + sel, :] = lax.dot_general(hot, attn_ref[...], (((0,), (0,)), ((), ())), preferred_element_type=F32).astype(BF16)
    lhs[rows + sel:rows + sel + own_rows, :] = attn_ref[pl.ds(pl.multiple_of(ids["tp"] * own_rows, own_rows), own_rows), :]
    base = (ids["lat"] * n_tp + ids["tp"]) * own_rows
    hot = (lax.broadcasted_iota(jnp.int32, (own_rows, sel), 0) + base == pos_ref[...]).astype(BF16)
    eye = (lax.broadcasted_iota(jnp.int32, (own_rows, own_rows), 0) == lax.broadcasted_iota(jnp.int32, (own_rows, own_rows), 1)).astype(BF16)
    pick_own[...] = lax.dot_general(hot, eye, (((0,), (0,)), ((), ())), preferred_element_type=F32).astype(BF16)

    def span(at, size):
        return pl.ds(pl.multiple_of(at, size), size)

    def exchange(rcv, send_sem, recv_sem, g, s, d):
        at = pl.ds(offs[s] + (d - 1) * sizes[s + 1], sizes[s + 1])
        sem = g * sem_at[-1] + sem_at[s] + d - 1
        return pltpu.make_async_remote_copy(
            src_ref=snd.at[g, at, :],
            dst_ref=rcv.at[g, at, :],
            send_sem=send_sem.at[sem],
            recv_sem=recv_sem.at[sem],
            device_id=peer(s, d),
            device_id_type=MESH,
        )

    tile = min(512, half_cols)
    per = tile // LANES

    def project(g, which):
        load(g, which).wait()
        if g == GROUPS - 1 and which == 0:
            for one in enc_loads:
                one.start()
        first = piece(g, which)

        def body(i, _):
            cols = pl.ds(pl.multiple_of(first + i * tile, tile), tile)
            out = jnp.dot(lhs[...], w_out[:, cols], preferred_element_type=F32)
            mix_snd[:, cols] = out[0:rows].astype(BF16)
            mix_own[:, cols] = out[rows + sel:]
            part = out[rows:rows + sel] + jnp.dot(pick_own[...], resid_ref[:, cols], preferred_element_type=F32)
            for k in range(per):
                block = part[:, k * LANES:(k + 1) * LANES]
                at = (i * per + k) * sel
                if which == 0:
                    snd[g, pl.ds(pl.multiple_of(at, sel), sel), :] = block.astype(BF16)
                else:
                    acc[pl.ds(pl.multiple_of(g * rg + core * (rg // 2) + at, sel), sel), :] = block
            return 0

        lax.fori_loop(0, half_cols // tile, body, 0, unroll=True)
        if which == 0:
            if g == 0:
                pl.semaphore_wait(barrier, len(peers))
            exchange(rcv_a, a_send, a_recv, g, 0, 1).start()

    def take(rcv, send_sem, recv_sem, last, g, s):
        radix = steps[s][2]
        for d in range(1, radix):
            exchange(rcv, send_sem, recv_sem, g, s, d).wait_recv()

        def total(at, size):
            out = acc[span(g * rg + start[s + 1] + at, size), :]
            for d in range(1, radix):
                out = out + rcv[g, span(offs[s] + (d - 1) * sizes[s + 1] + at, size), :].astype(F32)
            return out

        if s + 1 == n_steps:
            last(g, total(0, sizes[s + 1]))
            return
        size = sizes[s + 2]
        for d in range(1, steps[s + 1][2]):
            snd[g, pl.ds(offs[s + 1] + (d - 1) * size, size), :] = total(towards(s + 1, d) * size, size).astype(BF16)
            exchange(rcv, send_sem, recv_sem, g, s + 1, d).start()
        acc[span(g * rg + start[s + 2], size), :] = total(digit[s + 1] * size, size)

    def sent(rcv, send_sem, recv_sem):
        for g in range(GROUPS):
            for s in range(n_steps):
                for d in range(1, steps[s][2]):
                    exchange(rcv, send_sem, recv_sem, g, s, d).wait_send()

    def share(g, s, d):
        at = span(g * rg + start[s + 1], sizes[s + 1])
        sem = g * sem_at[-1] + sem_at[s] + d - 1
        return pltpu.make_async_remote_copy(
            src_ref=pk.at[at, :],
            dst_ref=pk.at[at, :],
            send_sem=g_send.at[sem],
            recv_sem=g_recv.at[sem],
            device_id=peer(s, d),
            device_id_type=MESH,
        )

    def share_start(g, s):
        for d in range(1, steps[s][2]):
            share(g, s, d).start()

    def share_take(g, s):
        for d in range(1, steps[s][2]):
            share(g, s, d).wait_recv()

    def own_rows_done(g, total):
        pk[span(g * rg + start[n_steps], sizes[n_steps]), :] = total.astype(BF16)
        share_start(g, n_steps - 1)

    n_tile = min(256, pre.shape[1])

    def encode(g, at, size):
        count = size // sel
        first = g * cg + lax.div(at, sel)
        parts = []
        for k in range(count):
            ct = first + k
            block = pk[pl.ds(pl.multiple_of(ct * sel, sel), sel), :].astype(F32)
            acc[pl.ds(pl.multiple_of(ct * sel, sel), sel), :] = block
            parts.append((block - bdec_ref[pl.ds(ct, 1), :]).astype(BF16))
        left = jnp.concatenate(parts, axis=1)
        deep = pl.ds(pl.multiple_of(first * LANES, count * LANES), count * LANES)

        def body(i, _):
            cols = pl.ds(pl.multiple_of(i * n_tile, n_tile), n_tile)
            pre[:, cols] += jnp.dot(left, w_enc[deep, cols], preferred_element_type=F32)
            return 0

        lax.fori_loop(0, pre.shape[1] // n_tile, body, 0, unroll=True)

    def mix(d):
        to = mix_peer(d)
        return pltpu.make_async_remote_copy(
            src_ref=mix_snd.at[pl.ds(pl.multiple_of(to * own_rows, own_rows), own_rows), :],
            dst_ref=mix_rcv.at[d - 1],
            send_sem=m_send.at[d - 1],
            recv_sem=m_recv.at[d - 1],
            device_id={"tp": to},
            device_id_type=MESH,
        )

    def wave(ops, after=None):
        for t in range(len(ops) + GROUPS - 1):
            for g in reversed(range(GROUPS)):
                if 0 <= t - g < len(ops):
                    ops[t - g](g)
            if after is not None:
                after(t)

    def encode_near(g):
        share_take(g, 1)
        share_start(g, 0)
        if g == GROUPS - 1:
            for d in range(1, n_tp):
                mix(d).start()
        if g == 0:
            for one in enc_loads:
                one.wait()
        encode(g, start[1], rg // 2)

    def encode_far(g):
        share_take(g, 0)
        encode(g, (1 - core) * (rg // 2), rg // 2)

    def pass_on(g, s):
        share_take(g, s)
        share_start(g, s - 1)

    pre[...] = jnp.zeros_like(pre)
    ops = [functools.partial(project, which=0), functools.partial(project, which=1)]
    ops += [functools.partial(take, rcv_a, a_send, a_recv, own_rows_done, s=s) for s in range(n_steps)]
    ops += [functools.partial(pass_on, s=s) for s in reversed(range(2, n_steps))]
    ops += [encode_near, encode_far]
    wave(ops)
    sent(rcv_a, a_send, a_recv)
    for g in range(GROUPS):
        for s in range(n_steps):
            for d in range(1, steps[s][2]):
                share(g, s, d).wait_send()

    codes = (jnp.maximum(pre[...] + b_enc_ref[...], 0.0) * norm_ref[...]).astype(BF16)
    codes_ref[...] = codes

    keep = sel // n_dev
    me = ids["tp"] * n_lat + ids["lat"]
    for r in range(keep):
        mine[r] = acc[pl.ds(me * keep + r, width // LANES, stride=sel), :]

    q = lax.broadcasted_iota(jnp.int32, (sel, sel), 0)
    row = lax.rem(q, keep)
    for s, (axis, low, radix) in enumerate(steps):
        weight = keep * (1 << low) * (n_lat if axis == "tp" else 1)
        row = row + lax.rem(lax.div(q, sizes[s + 1] // cg), radix) * weight
    turn = (row == lax.broadcasted_iota(jnp.int32, (sel, sel), 1)).astype(BF16)
    cperm[...] = jnp.dot(turn, codes, preferred_element_type=F32).astype(BF16)
    d_tile = min(256, cg * LANES)
    d_per = d_tile // LANES

    def decode(g):
        left = cperm[...]

        def body(i, _):
            at = pl.ds(pl.multiple_of(g * cg * LANES + i * d_tile, d_tile), d_tile)
            out = lax.dot_general(left, w_enc[at, :], (((1,), (1,)), ((), ())), preferred_element_type=F32)
            for k in range(d_per):
                acc[pl.ds(g * rg + i * d_per + k, sel, stride=cg), :] = out[:, k * LANES:(k + 1) * LANES]
            return 0

        lax.fori_loop(0, cg * LANES // d_tile, body, 0, unroll=True)
        half = rg // 2
        snd[g, pl.ds(0, half), :] = acc[span(g * rg + (1 - core) * half, half), :].astype(BF16)
        exchange(rcv_c, c_send, c_recv, g, 0, 1).start()

    sums = [None] * keep

    def score(g, total):
        for r in range(keep):
            full = total[r * cg:(r + 1) * cg] + bdec_ref[g * cg:(g + 1) * cg, :]
            recon_ref[r * (width // LANES) + g * cg:r * (width // LANES) + (g + 1) * cg, :] = full
            off = full - mine[r, g * cg:(g + 1) * cg, :]
            sums[r] = off * off if sums[r] is None else sums[r] + off * off

    def keep_stream(t):
        if t != GROUPS:
            return
        for d in range(1, n_tp):
            mix(d).wait_recv()

        def body(i, _):
            cols = pl.ds(pl.multiple_of(i * 1024, 1024), 1024)
            total = mix_own[:, cols]
            for d in range(1, n_tp):
                total = total + mix_rcv[d - 1, :, cols].astype(F32)
            stream_ref[:, cols] = (resid_ref[:, cols].astype(F32) + total).astype(BF16)
            return 0

        lax.fori_loop(0, width // 1024, body, 0)

    ops = [decode] + [functools.partial(take, rcv_c, c_send, c_recv, score, s=s) for s in range(n_steps)]
    wave(ops, keep_stream)
    for r in range(keep):
        total = jnp.sum(jnp.sum(sums[r], axis=0, keepdims=True), axis=1, keepdims=True) / width
        err_ref[r:r + 1, :] = jnp.broadcast_to(total, (1, LANES))
    sent(rcv_c, c_send, c_recv)
    for d in range(1, n_tp):
        mix(d).wait_send()


def finish(stream_in, codes_in, recon_in, err_in, stream_ref, codes_ref, recon_ref, err_ref):
    stream_ref[...] = stream_in[...]
    codes_ref[...] = codes_in[...]
    keep, width = recon_ref.shape
    feats = width // LANES
    for c in range(feats):
        recon_ref[:, c * LANES:(c + 1) * LANES] = recon_in[pl.ds(c, keep, stride=feats), :].astype(BF16)
    for r in range(keep):
        err_ref[r] = err_in[r, 0]


def shards(attn_out, w_out, resid_in, positions, w_enc, b_enc, dec_norm, b_dec):
    n_tp = lax.axis_size("tp")
    n_lat = lax.axis_size("lat")
    n_dev = n_tp * n_lat
    rows, depth = attn_out.shape
    own_rows, width = resid_in.shape
    sel = positions.shape[0]
    lats = w_enc.shape[1]
    keep = sel // n_dev
    feats = width // LANES
    rg = feats // GROUPS * sel
    n_sem = GROUPS * sum(radix - 1 for _, _, radix in digits(n_tp, n_lat))
    vmem = pl.BlockSpec(memory_space=pltpu.VMEM)
    hbm = pl.BlockSpec(memory_space=pl.ANY)
    dma = pltpu.SemaphoreType.DMA
    made = pl.pallas_call(
        functools.partial(kernel, n_tp, n_lat),
        out_shape=(
            jax.ShapeDtypeStruct((own_rows, width), BF16),
            jax.ShapeDtypeStruct((sel, lats), BF16),
            jax.ShapeDtypeStruct((keep * feats, LANES), F32),
            jax.ShapeDtypeStruct((keep, LANES), F32),
        ),
        in_specs=[vmem] * 6 + [hbm] * 2,
        out_specs=(vmem,) * 4,
        scratch_shapes=[
            pltpu.VMEM((depth, width), BF16),
            pltpu.VMEM((width, lats), BF16),
            pltpu.VMEM((rows + sel + own_rows, depth), BF16),
            pltpu.VMEM((sel, own_rows), BF16),
            pltpu.VMEM((GROUPS * rg, LANES), F32),
            pltpu.VMEM((GROUPS * rg, LANES), BF16),
            pltpu.VMEM((GROUPS, rg, LANES), BF16),
            pltpu.VMEM((GROUPS, rg, LANES), BF16),
            pltpu.VMEM((GROUPS, rg, LANES), BF16),
            pltpu.VMEM((rows, width), BF16),
            pltpu.VMEM((n_tp - 1, own_rows, width), BF16),
            pltpu.VMEM((own_rows, width), F32),
            pltpu.VMEM((sel, lats), F32),
            pltpu.VMEM((sel, lats), BF16),
            pltpu.VMEM((keep, feats, LANES), F32),
            dma((2 * GROUPS,)),
            dma((8,)),
            dma((n_sem,)), dma((n_sem,)),
            dma((n_sem,)), dma((n_sem,)),
            dma((n_sem,)), dma((n_sem,)),
            dma((n_tp - 1,)), dma((n_tp - 1,)),
        ],
        compiler_params=pltpu.CompilerParams(
            collective_id=0, has_side_effects=True, vmem_limit_bytes=60 * 1024 * 1024
        ),
        cost_estimate=pl.CostEstimate(
            flops=2 * (2 * sel * width * lats + (rows + sel + own_rows) * depth * width),
            bytes_accessed=2 * (w_out.size + w_enc.size),
            transcendentals=0,
        ),
    )(
        positions.reshape(1, sel),
        attn_out,
        resid_in,
        b_enc.reshape(1, lats),
        dec_norm.reshape(1, lats),
        b_dec.reshape(feats, LANES),
        w_out,
        w_enc,
    )
    smem = pl.BlockSpec(memory_space=pltpu.SMEM)
    return pl.pallas_call(
        finish,
        out_shape=(
            jax.ShapeDtypeStruct((own_rows, width), BF16),
            jax.ShapeDtypeStruct((sel, lats), BF16),
            jax.ShapeDtypeStruct((keep, width), BF16),
            jax.ShapeDtypeStruct((keep,), F32),
        ),
        in_specs=[vmem] * 3 + [smem],
        out_specs=(vmem,) * 3 + (smem,),
    )(*made)


def solution(mesh):
    placed = (
        P("lat", "tp"),
        P("tp", None),
        P(("lat", "tp"), None),
        P(),
        P(None, ("tp", "lat")),
        P(("tp", "lat")),
        P(("tp", "lat")),
        P(),
    )
    return jax.shard_map(
        shards,
        mesh=mesh,
        in_specs=placed,
        out_specs=(
            P(("lat", "tp"), None),
            P(None, ("tp", "lat")),
            P(("tp", "lat"), None),
            P(("tp", "lat")),
        ),
        check_vma=False,
    )
```

```python
import functools

import jax
import jax.numpy as jnp
from jax import lax
from jax.experimental import pallas as pl
from jax.experimental.pallas import tpu as pltpu
from jax.sharding import PartitionSpec as P

GROUPS = 2
LANES = 128
F32 = jnp.float32
BF16 = jnp.bfloat16
MESH = pl.DeviceIdType.MESH


def log2(n):
    return n.bit_length() - 1


def digits(n_tp, n_lat):
    tp_bits, lat_bits = log2(n_tp), log2(n_lat)
    out = [("lat", 0, 2)] if lat_bits else []
    out += [("tp", b, 1 << min(2, tp_bits - b)) for b in range(0, tp_bits, 2)]
    out += [("lat", b, 1 << min(2, lat_bits - b)) for b in range(1, lat_bits, 2)]
    return out


def kernel(n_tp, n_lat, pos_ref, attn_ref, resid_ref, b_enc_ref, norm_ref, bdec_ref, w_out_hbm, w_enc_hbm,
           stream_ref, codes_ref, recon_ref, err_ref,
           w_out, w_enc, lhs, pick_own, acc, pk, snd, rcv_a, rcv_c, mix_snd, mix_rcv, mix_own, pre, cperm, mine,
           in_sem, enc_sem, a_send, a_recv, g_send, g_recv, c_send, c_recv, m_send, m_recv):
    ids = {"tp": lax.axis_index("tp"), "lat": lax.axis_index("lat")}
    n_dev = n_tp * n_lat
    rows, depth = attn_ref.shape
    own_rows, width = resid_ref.shape
    sel = pos_ref.shape[1]
    cg = width // LANES // GROUPS
    rg = cg * sel
    steps = digits(n_tp, n_lat)
    n_steps = len(steps)
    digit = [lax.rem(lax.div(ids[axis], 1 << low), radix) for axis, low, radix in steps]
    sizes = [rg]
    for axis, low, radix in steps:
        sizes.append(sizes[-1] // radix)
    offs = [0]
    sem_at = [0]
    for s in range(n_steps):
        offs.append(offs[-1] + (steps[s][2] - 1) * sizes[s + 1])
        sem_at.append(sem_at[-1] + steps[s][2] - 1)
    start = [0]
    for s in range(n_steps):
        start.append(start[-1] + digit[s] * sizes[s + 1])

    def towards(s, d):
        return lax.rem(digit[s] + d, steps[s][2])

    def peer(s, d):
        axis, low, radix = steps[s]
        return {axis: ids[axis] + (towards(s, d) - digit[s]) * (1 << low)}

    core = digit[0]
    half_cols = cg * LANES // 2

    def piece(g, which):
        h = 1 - core if which == 0 else core
        return pl.multiple_of(g * cg * LANES + h * half_cols, half_cols)

    def load(g, which):
        cols = pl.ds(piece(g, which), half_cols)
        return pltpu.make_async_copy(w_out_hbm.at[:, cols], w_out.at[:, cols], in_sem.at[which * GROUPS + g])

    load(0, 0).start()
    for g in range(GROUPS):
        if g + 1 < GROUPS:
            load(g + 1, 0).start()
        load(g, 1).start()
    n_enc = enc_sem.shape[0]
    enc_rows = width // n_enc
    enc_loads = [
        pltpu.make_async_copy(w_enc_hbm.at[pl.ds(i * enc_rows, enc_rows), :], w_enc.at[pl.ds(i * enc_rows, enc_rows), :], enc_sem.at[i])
        for i in range(n_enc)
    ]

    barrier = pltpu.get_barrier_semaphore()
    mix_peer = lambda d: lax.rem(ids["tp"] + d, n_tp)
    peers = [peer(s, d) for s in range(n_steps) if steps[s][0] == "lat" for d in range(1, steps[s][2])]
    peers += [{"tp": mix_peer(d)} for d in range(1, n_tp)]
    for one in peers:
        pl.semaphore_signal(barrier, inc=1, device_id=one, device_id_type=MESH)

    base = ids["lat"] * rows
    hot = (lax.broadcasted_iota(jnp.int32, (rows, sel), 0) + base == pos_ref[...]).astype(BF16)
    lhs[0:rows, :] = attn_ref[...]
    lhs[rows:rows + sel, :] = lax.dot_general(hot, attn_ref[...], (((0,), (0,)), ((), ())), preferred_element_type=F32).astype(BF16)
    lhs[rows + sel:rows + sel + own_rows, :] = attn_ref[pl.ds(pl.multiple_of(ids["tp"] * own_rows, own_rows), own_rows), :]
    base = (ids["lat"] * n_tp + ids["tp"]) * own_rows
    hot = (lax.broadcasted_iota(jnp.int32, (own_rows, sel), 0) + base == pos_ref[...]).astype(BF16)
    eye = (lax.broadcasted_iota(jnp.int32, (own_rows, own_rows), 0) == lax.broadcasted_iota(jnp.int32, (own_rows, own_rows), 1)).astype(BF16)
    pick_own[...] = lax.dot_general(hot, eye, (((0,), (0,)), ((), ())), preferred_element_type=F32).astype(BF16)

    def span(at, size):
        return pl.ds(pl.multiple_of(at, size), size)

    def exchange(rcv, send_sem, recv_sem, g, s, d):
        at = pl.ds(offs[s] + (d - 1) * sizes[s + 1], sizes[s + 1])
        sem = g * sem_at[-1] + sem_at[s] + d - 1
        return pltpu.make_async_remote_copy(
            src_ref=snd.at[g, at, :],
            dst_ref=rcv.at[g, at, :],
            send_sem=send_sem.at[sem],
            recv_sem=recv_sem.at[sem],
            device_id=peer(s, d),
            device_id_type=MESH,
        )

    tile = min(512, half_cols)
    per = tile // LANES

    def project(g, which):
        load(g, which).wait()
        if g == GROUPS - 1 and which == 0:
            for one in enc_loads:
                one.start()
        first = piece(g, which)

        def body(i, _):
            cols = pl.ds(pl.multiple_of(first + i * tile, tile), tile)
            out = jnp.dot(lhs[...], w_out[:, cols], preferred_element_type=F32)
            mix_snd[:, cols] = out[0:rows].astype(BF16)
            mix_own[:, cols] = out[rows + sel:]
            part = out[rows:rows + sel] + jnp.dot(pick_own[...], resid_ref[:, cols], preferred_element_type=F32)
            for k in range(per):
                block = part[:, k * LANES:(k + 1) * LANES]
                at = (i * per + k) * sel
                if which == 0:
                    snd[g, pl.ds(pl.multiple_of(at, sel), sel), :] = block.astype(BF16)
                else:
                    acc[pl.ds(pl.multiple_of(g * rg + core * (rg // 2) + at, sel), sel), :] = block
            return 0

        lax.fori_loop(0, half_cols // tile, body, 0, unroll=True)
        if which == 0:
            if g == 0:
                pl.semaphore_wait(barrier, len(peers))
            exchange(rcv_a, a_send, a_recv, g, 0, 1).start()

    def take(rcv, send_sem, recv_sem, last, g, s):
        radix = steps[s][2]
        for d in range(1, radix):
            exchange(rcv, send_sem, recv_sem, g, s, d).wait_recv()

        def total(at, size):
            out = acc[span(g * rg + start[s + 1] + at, size), :]
            for d in range(1, radix):
                out = out + rcv[g, span(offs[s] + (d - 1) * sizes[s + 1] + at, size), :].astype(F32)
            return out

        if s + 1 == n_steps:
            last(g, total(0, sizes[s + 1]))
            return
        size = sizes[s + 2]
        for d in range(1, steps[s + 1][2]):
            snd[g, pl.ds(offs[s + 1] + (d - 1) * size, size), :] = total(towards(s + 1, d) * size, size).astype(BF16)
            exchange(rcv, send_sem, recv_sem, g, s + 1, d).start()
        acc[span(g * rg + start[s + 2], size), :] = total(digit[s + 1] * size, size)

    def sent(rcv, send_sem, recv_sem):
        for g in range(GROUPS):
            for s in range(n_steps):
                for d in range(1, steps[s][2]):
                    exchange(rcv, send_sem, recv_sem, g, s, d).wait_send()

    def share(g, s, d):
        at = span(g * rg + start[s + 1], sizes[s + 1])
        sem = g * sem_at[-1] + sem_at[s] + d - 1
        return pltpu.make_async_remote_copy(
            src_ref=pk.at[at, :],
            dst_ref=pk.at[at, :],
            send_sem=g_send.at[sem],
            recv_sem=g_recv.at[sem],
            device_id=peer(s, d),
            device_id_type=MESH,
        )

    def share_start(g, s):
        for d in range(1, steps[s][2]):
            share(g, s, d).start()

    def share_take(g, s):
        for d in range(1, steps[s][2]):
            share(g, s, d).wait_recv()

    def own_rows_done(g, total):
        pk[span(g * rg + start[n_steps], sizes[n_steps]), :] = total.astype(BF16)
        share_start(g, n_steps - 1)

    n_tile = min(256, pre.shape[1])

    def encode(g, at, size):
        count = size // sel
        first = g * cg + lax.div(at, sel)
        parts = []
        for k in range(count):
            ct = first + k
            block = pk[pl.ds(pl.multiple_of(ct * sel, sel), sel), :].astype(F32)
            acc[pl.ds(pl.multiple_of(ct * sel, sel), sel), :] = block
            parts.append((block - bdec_ref[pl.ds(ct, 1), :]).astype(BF16))
        left = jnp.concatenate(parts, axis=1)
        deep = pl.ds(pl.multiple_of(first * LANES, count * LANES), count * LANES)

        def body(i, _):
            cols = pl.ds(pl.multiple_of(i * n_tile, n_tile), n_tile)
            pre[:, cols] += jnp.dot(left, w_enc[deep, cols], preferred_element_type=F32)
            return 0

        lax.fori_loop(0, pre.shape[1] // n_tile, body, 0, unroll=True)

    def mix(d):
        to = mix_peer(d)
        return pltpu.make_async_remote_copy(
            src_ref=mix_snd.at[pl.ds(pl.multiple_of(to * own_rows, own_rows), own_rows), :],
            dst_ref=mix_rcv.at[d - 1],
            send_sem=m_send.at[d - 1],
            recv_sem=m_recv.at[d - 1],
            device_id={"tp": to},
            device_id_type=MESH,
        )

    def wave(ops, after=None):
        for t in range(len(ops) + GROUPS - 1):
            for g in reversed(range(GROUPS)):
                if 0 <= t - g < len(ops):
                    ops[t - g](g)
            if after is not None:
                after(t)

    def encode_near(g):
        share_take(g, 1)
        share_start(g, 0)
        if g == GROUPS - 1:
            for d in range(1, n_tp):
                mix(d).start()
        if g == 0:
            for one in enc_loads:
                one.wait()
        encode(g, start[1], rg // 2)

    def encode_far(g):
        share_take(g, 0)
        encode(g, (1 - core) * (rg // 2), rg // 2)

    def pass_on(g, s):
        share_take(g, s)
        share_start(g, s - 1)

    pre[...] = jnp.zeros_like(pre)
    ops = [functools.partial(project, which=0), functools.partial(project, which=1)]
    ops += [functools.partial(take, rcv_a, a_send, a_recv, own_rows_done, s=s) for s in range(n_steps)]
    ops += [functools.partial(pass_on, s=s) for s in reversed(range(2, n_steps))]
    ops += [encode_near, encode_far]
    wave(ops)
    sent(rcv_a, a_send, a_recv)
    for g in range(GROUPS):
        for s in range(n_steps):
            for d in range(1, steps[s][2]):
                share(g, s, d).wait_send()

    codes = (jnp.maximum(pre[...] + b_enc_ref[...], 0.0) * norm_ref[...]).astype(BF16)
    codes_ref[...] = codes

    keep = sel // n_dev
    me = ids["tp"] * n_lat + ids["lat"]
    for r in range(keep):
        mine[r] = acc[pl.ds(me * keep + r, width // LANES, stride=sel), :]

    q = lax.broadcasted_iota(jnp.int32, (sel, sel), 0)
    row = lax.rem(q, keep)
    for s, (axis, low, radix) in enumerate(steps):
        weight = keep * (1 << low) * (n_lat if axis == "tp" else 1)
        row = row + lax.rem(lax.div(q, sizes[s + 1] // cg), radix) * weight
    turn = (row == lax.broadcasted_iota(jnp.int32, (sel, sel), 1)).astype(BF16)
    cperm[...] = jnp.dot(turn, codes, preferred_element_type=F32).astype(BF16)
    d_tile = min(256, cg * LANES)
    d_per = d_tile // LANES

    def decode(g):
        left = cperm[...]

        def body(i, _):
            at = pl.ds(pl.multiple_of(g * cg * LANES + i * d_tile, d_tile), d_tile)
            out = lax.dot_general(left, w_enc[at, :], (((1,), (1,)), ((), ())), preferred_element_type=F32)
            for k in range(d_per):
                acc[pl.ds(g * rg + i * d_per + k, sel, stride=cg), :] = out[:, k * LANES:(k + 1) * LANES]
            return 0

        lax.fori_loop(0, cg * LANES // d_tile, body, 0, unroll=True)
        half = rg // 2
        snd[g, pl.ds(0, half), :] = acc[span(g * rg + (1 - core) * half, half), :].astype(BF16)
        exchange(rcv_c, c_send, c_recv, g, 0, 1).start()

    sums = [None] * keep

    def score(g, total):
        for r in range(keep):
            full = total[r * cg:(r + 1) * cg] + bdec_ref[g * cg:(g + 1) * cg, :]
            recon_ref[r * (width // LANES) + g * cg:r * (width // LANES) + (g + 1) * cg, :] = full
            off = full - mine[r, g * cg:(g + 1) * cg, :]
            sums[r] = off * off if sums[r] is None else sums[r] + off * off

    def keep_stream(t):
        if t != GROUPS:
            return
        for d in range(1, n_tp):
            mix(d).wait_recv()

        def body(i, _):
            cols = pl.ds(pl.multiple_of(i * 1024, 1024), 1024)
            total = mix_own[:, cols]
            for d in range(1, n_tp):
                total = total + mix_rcv[d - 1, :, cols].astype(F32)
            stream_ref[:, cols] = (resid_ref[:, cols].astype(F32) + total).astype(BF16)
            return 0

        lax.fori_loop(0, width // 1024, body, 0)

    ops = [decode] + [functools.partial(take, rcv_c, c_send, c_recv, score, s=s) for s in range(n_steps)]
    wave(ops, keep_stream)
    for r in range(keep):
        total = jnp.sum(jnp.sum(sums[r], axis=0, keepdims=True), axis=1, keepdims=True) / width
        err_ref[r:r + 1, :] = jnp.broadcast_to(total, (1, LANES))
    sent(rcv_c, c_send, c_recv)
    for d in range(1, n_tp):
        mix(d).wait_send()


def finish(stream_in, codes_in, recon_in, err_in, stream_ref, codes_ref, recon_ref, err_ref):
    stream_ref[...] = stream_in[...]
    codes_ref[...] = codes_in[...]
    keep, width = recon_ref.shape
    feats = width // LANES
    for c in range(feats):
        recon_ref[:, c * LANES:(c + 1) * LANES] = recon_in[pl.ds(c, keep, stride=feats), :].astype(BF16)
    for r in range(keep):
        err_ref[r] = err_in[r, 0]


def shards(attn_out, w_out, resid_in, positions, w_enc, b_enc, dec_norm, b_dec):
    n_tp = lax.axis_size("tp")
    n_lat = lax.axis_size("lat")
    n_dev = n_tp * n_lat
    rows, depth = attn_out.shape
    own_rows, width = resid_in.shape
    sel = positions.shape[0]
    lats = w_enc.shape[1]
    keep = sel // n_dev
    feats = width // LANES
    rg = feats // GROUPS * sel
    n_sem = GROUPS * sum(radix - 1 for _, _, radix in digits(n_tp, n_lat))
    vmem = pl.BlockSpec(memory_space=pltpu.VMEM)
    hbm = pl.BlockSpec(memory_space=pl.ANY)
    dma = pltpu.SemaphoreType.DMA
    made = pl.pallas_call(
        functools.partial(kernel, n_tp, n_lat),
        out_shape=(
            jax.ShapeDtypeStruct((own_rows, width), BF16),
            jax.ShapeDtypeStruct((sel, lats), BF16),
            jax.ShapeDtypeStruct((keep * feats, LANES), F32),
            jax.ShapeDtypeStruct((keep, LANES), F32),
        ),
        in_specs=[vmem] * 6 + [hbm] * 2,
        out_specs=(vmem,) * 4,
        scratch_shapes=[
            pltpu.VMEM((depth, width), BF16),
            pltpu.VMEM((width, lats), BF16),
            pltpu.VMEM((rows + sel + own_rows, depth), BF16),
            pltpu.VMEM((sel, own_rows), BF16),
            pltpu.VMEM((GROUPS * rg, LANES), F32),
            pltpu.VMEM((GROUPS * rg, LANES), BF16),
            pltpu.VMEM((GROUPS, rg, LANES), BF16),
            pltpu.VMEM((GROUPS, rg, LANES), BF16),
            pltpu.VMEM((GROUPS, rg, LANES), BF16),
            pltpu.VMEM((rows, width), BF16),
            pltpu.VMEM((n_tp - 1, own_rows, width), BF16),
            pltpu.VMEM((own_rows, width), F32),
            pltpu.VMEM((sel, lats), F32),
            pltpu.VMEM((sel, lats), BF16),
            pltpu.VMEM((keep, feats, LANES), F32),
            dma((2 * GROUPS,)),
            dma((8,)),
            dma((n_sem,)), dma((n_sem,)),
            dma((n_sem,)), dma((n_sem,)),
            dma((n_sem,)), dma((n_sem,)),
            dma((n_tp - 1,)), dma((n_tp - 1,)),
        ],
        compiler_params=pltpu.CompilerParams(
            collective_id=0, has_side_effects=True, vmem_limit_bytes=57 * 1024 * 1024
        ),
        cost_estimate=pl.CostEstimate(
            flops=2 * (2 * sel * width * lats + (rows + sel + own_rows) * depth * width),
            bytes_accessed=2 * (w_out.size + w_enc.size),
            transcendentals=0,
        ),
    )(
        positions.reshape(1, sel),
        attn_out,
        resid_in,
        b_enc.reshape(1, lats),
        dec_norm.reshape(1, lats),
        b_dec.reshape(feats, LANES),
        w_out,
        w_enc,
    )
    smem = pl.BlockSpec(memory_space=pltpu.SMEM)
    return pl.pallas_call(
        finish,
        out_shape=(
            jax.ShapeDtypeStruct((own_rows, width), BF16),
            jax.ShapeDtypeStruct((sel, lats), BF16),
            jax.ShapeDtypeStruct((keep, width), BF16),
            jax.ShapeDtypeStruct((keep,), F32),
        ),
        in_specs=[vmem] * 3 + [smem],
        out_specs=(vmem,) * 3 + (smem,),
    )(*made)


def solution(mesh):
    placed = (
        P("lat", "tp"),
        P("tp", None),
        P(("lat", "tp"), None),
        P(),
        P(None, ("tp", "lat")),
        P(("tp", "lat")),
        P(("tp", "lat")),
        P(),
    )
    return jax.shard_map(
        shards,
        mesh=mesh,
        in_specs=placed,
        out_specs=(
            P(("lat", "tp"), None),
            P(None, ("tp", "lat")),
            P(("tp", "lat"), None),
            P(("tp", "lat")),
        ),
        check_vma=False,
    )
```

```python
import functools

import jax
import jax.numpy as jnp
from jax import lax
from jax.experimental import pallas as pl
from jax.experimental.pallas import tpu as pltpu
from jax.sharding import PartitionSpec as P

GROUPS = 2
LANES = 128
F32 = jnp.float32
BF16 = jnp.bfloat16
MESH = pl.DeviceIdType.MESH


def log2(n):
    return n.bit_length() - 1


def digits(n_tp, n_lat):
    tp_bits, lat_bits = log2(n_tp), log2(n_lat)
    out = [("lat", 0, 2)] if lat_bits else []
    out += [("tp", b, 1 << min(2, tp_bits - b)) for b in range(0, tp_bits, 2)]
    out += [("lat", b, 1 << min(2, lat_bits - b)) for b in range(1, lat_bits, 2)]
    return out


def kernel(n_tp, n_lat, pos_ref, attn_ref, resid_ref, b_enc_ref, norm_ref, bdec_ref, w_out_hbm, w_enc_hbm,
           stream_ref, codes_ref, recon_ref, err_ref,
           w_out, w_enc, lhs, pick_own, acc, pk, snd, rcv_a, rcv_c, mix_snd, mix_rcv, mix_own, pre, cperm, mine,
           in_sem, enc_sem, a_send, a_recv, g_send, g_recv, c_send, c_recv, m_send, m_recv):
    ids = {"tp": lax.axis_index("tp"), "lat": lax.axis_index("lat")}
    n_dev = n_tp * n_lat
    rows, depth = attn_ref.shape
    own_rows, width = resid_ref.shape
    sel = pos_ref.shape[1]
    cg = width // LANES // GROUPS
    rg = cg * sel
    steps = digits(n_tp, n_lat)
    n_steps = len(steps)
    digit = [lax.rem(lax.div(ids[axis], 1 << low), radix) for axis, low, radix in steps]
    sizes = [rg]
    for axis, low, radix in steps:
        sizes.append(sizes[-1] // radix)
    offs = [0]
    sem_at = [0]
    for s in range(n_steps):
        offs.append(offs[-1] + (steps[s][2] - 1) * sizes[s + 1])
        sem_at.append(sem_at[-1] + steps[s][2] - 1)
    start = [0]
    for s in range(n_steps):
        start.append(start[-1] + digit[s] * sizes[s + 1])

    def towards(s, d):
        return lax.rem(digit[s] + d, steps[s][2])

    def peer(s, d):
        axis, low, radix = steps[s]
        return {axis: ids[axis] + (towards(s, d) - digit[s]) * (1 << low)}

    core = digit[0]
    half_cols = cg * LANES // 2

    def piece(g, which):
        h = 1 - core if which == 0 else core
        return pl.multiple_of(g * cg * LANES + h * half_cols, half_cols)

    def load(g, which):
        cols = pl.ds(piece(g, which), half_cols)
        return pltpu.make_async_copy(w_out_hbm.at[:, cols], w_out.at[:, cols], in_sem.at[which * GROUPS + g])

    load(0, 0).start()
    for g in range(GROUPS):
        if g + 1 < GROUPS:
            load(g + 1, 0).start()
        load(g, 1).start()
    n_enc = enc_sem.shape[0]
    enc_rows = width // n_enc
    enc_loads = [
        pltpu.make_async_copy(w_enc_hbm.at[pl.ds(i * enc_rows, enc_rows), :], w_enc.at[pl.ds(i * enc_rows, enc_rows), :], enc_sem.at[i])
        for i in range(n_enc)
    ]

    barrier = pltpu.get_barrier_semaphore()
    mix_peer = lambda d: lax.rem(ids["tp"] + d, n_tp)
    peers = [peer(s, d) for s in range(n_steps) if steps[s][0] == "lat" for d in range(1, steps[s][2])]
    peers += [{"tp": mix_peer(d)} for d in range(1, n_tp)]
    for one in peers:
        pl.semaphore_signal(barrier, inc=1, device_id=one, device_id_type=MESH)

    base = ids["lat"] * rows
    hot = (lax.broadcasted_iota(jnp.int32, (rows, sel), 0) + base == pos_ref[...]).astype(BF16)
    lhs[0:rows, :] = attn_ref[...]
    lhs[rows:rows + sel, :] = lax.dot_general(hot, attn_ref[...], (((0,), (0,)), ((), ())), preferred_element_type=F32).astype(BF16)
    lhs[rows + sel:rows + sel + own_rows, :] = attn_ref[pl.ds(pl.multiple_of(ids["tp"] * own_rows, own_rows), own_rows), :]
    base = (ids["lat"] * n_tp + ids["tp"]) * own_rows
    hot = (lax.broadcasted_iota(jnp.int32, (own_rows, sel), 0) + base == pos_ref[...]).astype(BF16)
    eye = (lax.broadcasted_iota(jnp.int32, (own_rows, own_rows), 0) == lax.broadcasted_iota(jnp.int32, (own_rows, own_rows), 1)).astype(BF16)
    pick_own[...] = lax.dot_general(hot, eye, (((0,), (0,)), ((), ())), preferred_element_type=F32).astype(BF16)

    def span(at, size):
        return pl.ds(pl.multiple_of(at, size), size)

    def exchange(rcv, send_sem, recv_sem, g, s, d):
        at = pl.ds(offs[s] + (d - 1) * sizes[s + 1], sizes[s + 1])
        sem = g * sem_at[-1] + sem_at[s] + d - 1
        return pltpu.make_async_remote_copy(
            src_ref=snd.at[g, at, :],
            dst_ref=rcv.at[g, at, :],
            send_sem=send_sem.at[sem],
            recv_sem=recv_sem.at[sem],
            device_id=peer(s, d),
            device_id_type=MESH,
        )

    tile = min(512, half_cols)
    per = tile // LANES

    def project(g, which):
        load(g, which).wait()
        if g == GROUPS - 1 and which == 0:
            for one in enc_loads:
                one.start()
        first = piece(g, which)

        def body(i, _):
            cols = pl.ds(pl.multiple_of(first + i * tile, tile), tile)
            out = jnp.dot(lhs[...], w_out[:, cols], preferred_element_type=F32)
            mix_snd[:, cols] = out[0:rows].astype(BF16)
            mix_own[:, cols] = out[rows + sel:]
            part = out[rows:rows + sel] + jnp.dot(pick_own[...], resid_ref[:, cols], preferred_element_type=F32)
            for k in range(per):
                block = part[:, k * LANES:(k + 1) * LANES]
                at = (i * per + k) * sel
                if which == 0:
                    snd[g, pl.ds(pl.multiple_of(at, sel), sel), :] = block.astype(BF16)
                else:
                    acc[pl.ds(pl.multiple_of(g * rg + core * (rg // 2) + at, sel), sel), :] = block
            return 0

        lax.fori_loop(0, half_cols // tile, body, 0, unroll=True)
        if which == 0:
            if g == 0:
                pl.semaphore_wait(barrier, len(peers))
            exchange(rcv_a, a_send, a_recv, g, 0, 1).start()

    def take(rcv, send_sem, recv_sem, last, g, s):
        radix = steps[s][2]
        for d in range(1, radix):
            exchange(rcv, send_sem, recv_sem, g, s, d).wait_recv()

        def total(at, size):
            out = acc[span(g * rg + start[s + 1] + at, size), :]
            for d in range(1, radix):
                out = out + rcv[g, span(offs[s] + (d - 1) * sizes[s + 1] + at, size), :].astype(F32)
            return out

        if s + 1 == n_steps:
            last(g, total(0, sizes[s + 1]))
            return
        size = sizes[s + 2]
        for d in range(1, steps[s + 1][2]):
            snd[g, pl.ds(offs[s + 1] + (d - 1) * size, size), :] = total(towards(s + 1, d) * size, size).astype(BF16)
            exchange(rcv, send_sem, recv_sem, g, s + 1, d).start()
        acc[span(g * rg + start[s + 2], size), :] = total(digit[s + 1] * size, size)

    def sent(rcv, send_sem, recv_sem):
        for g in range(GROUPS):
            for s in range(n_steps):
                for d in range(1, steps[s][2]):
                    exchange(rcv, send_sem, recv_sem, g, s, d).wait_send()

    def share(g, s, d):
        at = span(g * rg + start[s + 1], sizes[s + 1])
        sem = g * sem_at[-1] + sem_at[s] + d - 1
        return pltpu.make_async_remote_copy(
            src_ref=pk.at[at, :],
            dst_ref=pk.at[at, :],
            send_sem=g_send.at[sem],
            recv_sem=g_recv.at[sem],
            device_id=peer(s, d),
            device_id_type=MESH,
        )

    def share_start(g, s):
        for d in range(1, steps[s][2]):
            share(g, s, d).start()

    def share_take(g, s):
        for d in range(1, steps[s][2]):
            share(g, s, d).wait_recv()

    def own_rows_done(g, total):
        pk[span(g * rg + start[n_steps], sizes[n_steps]), :] = total.astype(BF16)
        share_start(g, n_steps - 1)

    n_tile = min(256, pre.shape[1])

    def encode(g, at, size):
        count = size // sel
        first = g * cg + lax.div(at, sel)
        parts = []
        for k in range(count):
            ct = first + k
            block = pk[pl.ds(pl.multiple_of(ct * sel, sel), sel), :].astype(F32)
            acc[pl.ds(pl.multiple_of(ct * sel, sel), sel), :] = block
            parts.append((block - bdec_ref[pl.ds(ct, 1), :]).astype(BF16))
        left = jnp.concatenate(parts, axis=1)
        deep = pl.ds(pl.multiple_of(first * LANES, count * LANES), count * LANES)

        def body(i, _):
            cols = pl.ds(pl.multiple_of(i * n_tile, n_tile), n_tile)
            pre[:, cols] += jnp.dot(left, w_enc[deep, cols], preferred_element_type=F32)
            return 0

        lax.fori_loop(0, pre.shape[1] // n_tile, body, 0, unroll=True)

    mix_parts = (pl.ds(0, width // 4), pl.ds(width // 4, width - width // 4))

    def mix(part, d):
        to = mix_peer(d)
        sem = part * (n_tp - 1) + d - 1
        return pltpu.make_async_remote_copy(
            src_ref=mix_snd.at[pl.ds(pl.multiple_of(to * own_rows, own_rows), own_rows), mix_parts[part]],
            dst_ref=mix_rcv.at[d - 1, :, mix_parts[part]],
            send_sem=m_send.at[sem],
            recv_sem=m_recv.at[sem],
            device_id={"tp": to},
            device_id_type=MESH,
        )

    def mix_start(part):
        for d in range(1, n_tp):
            mix(part, d).start()

    def mix_early(t):
        if t == GROUPS + 2:
            mix_start(0)

    def wave(ops, after=None):
        for t in range(len(ops) + GROUPS - 1):
            for g in reversed(range(GROUPS)):
                if 0 <= t - g < len(ops):
                    ops[t - g](g)
            if after is not None:
                after(t)

    def encode_near(g):
        share_take(g, 1)
        share_start(g, 0)
        if g == GROUPS - 1:
            mix_start(1)
        if g == 0:
            for one in enc_loads:
                one.wait()
        encode(g, start[1], rg // 2)

    def encode_far(g):
        share_take(g, 0)
        encode(g, (1 - core) * (rg // 2), rg // 2)

    def pass_on(g, s):
        if g == GROUPS - 1 and s == n_steps - 1:
            sent(rcv_a, a_send, a_recv)
        share_take(g, s)
        share_start(g, s - 1)

    pre[...] = jnp.zeros_like(pre)
    ops = [functools.partial(project, which=0), functools.partial(project, which=1)]
    ops += [functools.partial(take, rcv_a, a_send, a_recv, own_rows_done, s=s) for s in range(n_steps)]
    ops += [functools.partial(pass_on, s=s) for s in reversed(range(2, n_steps))]
    ops += [encode_near, encode_far]
    wave(ops, mix_early)

    codes = (jnp.maximum(pre[...] + b_enc_ref[...], 0.0) * norm_ref[...]).astype(BF16)
    codes_ref[...] = codes

    keep = sel // n_dev
    me = ids["tp"] * n_lat + ids["lat"]
    for r in range(keep):
        mine[r] = acc[pl.ds(me * keep + r, width // LANES, stride=sel), :]

    q = lax.broadcasted_iota(jnp.int32, (sel, sel), 0)
    row = lax.rem(q, keep)
    for s, (axis, low, radix) in enumerate(steps):
        weight = keep * (1 << low) * (n_lat if axis == "tp" else 1)
        row = row + lax.rem(lax.div(q, sizes[s + 1] // cg), radix) * weight
    turn = (row == lax.broadcasted_iota(jnp.int32, (sel, sel), 1)).astype(BF16)
    cperm[...] = jnp.dot(turn, codes, preferred_element_type=F32).astype(BF16)
    d_tile = min(256, cg * LANES)
    d_per = d_tile // LANES

    d_count = cg * LANES // d_tile

    def decode(g, low, high):
        left = cperm[...]

        def body(i, _):
            at = pl.ds(pl.multiple_of(g * cg * LANES + i * d_tile, d_tile), d_tile)
            out = lax.dot_general(left, w_enc[at, :], (((1,), (1,)), ((), ())), preferred_element_type=F32)
            for k in range(d_per):
                acc[pl.ds(g * rg + i * d_per + k, sel, stride=cg), :] = out[:, k * LANES:(k + 1) * LANES]
            return 0

        lax.fori_loop(low, high, body, 0, unroll=True)
        if high < d_count:
            return
        half = rg // 2
        snd[g, pl.ds(0, half), :] = acc[span(g * rg + (1 - core) * half, half), :].astype(BF16)
        exchange(rcv_c, c_send, c_recv, g, 0, 1).start()

    sums = [None] * keep

    def score(g, total):
        for r in range(keep):
            full = total[r * cg:(r + 1) * cg] + bdec_ref[g * cg:(g + 1) * cg, :]
            recon_ref[r * (width // LANES) + g * cg:r * (width // LANES) + (g + 1) * cg, :] = full
            off = full - mine[r, g * cg:(g + 1) * cg, :]
            sums[r] = off * off if sums[r] is None else sums[r] + off * off

    def keep_stream():
        for part in range(len(mix_parts)):
            for d in range(1, n_tp):
                mix(part, d).wait_recv()

        def body(i, _):
            cols = pl.ds(pl.multiple_of(i * 1024, 1024), 1024)
            total = mix_own[:, cols]
            for d in range(1, n_tp):
                total = total + mix_rcv[d - 1, :, cols].astype(F32)
            stream_ref[:, cols] = (resid_ref[:, cols].astype(F32) + total).astype(BF16)
            return 0

        lax.fori_loop(0, width // 1024, body, 0)

    take_c = functools.partial(take, rcv_c, c_send, c_recv, score)
    decode(0, 0, d_count)
    for g in range(1, GROUPS):
        decode(g, 0, d_count // 2)
        take_c(g - 1, 0)
        decode(g, d_count // 2, d_count)
    take_c(GROUPS - 1, 0)
    for s in range(1, n_steps):
        if s == n_steps - 1:
            keep_stream()
        for g in range(GROUPS):
            take_c(g, s)
    for r in range(keep):
        total = jnp.sum(jnp.sum(sums[r], axis=0, keepdims=True), axis=1, keepdims=True) / width
        err_ref[r:r + 1, :] = jnp.broadcast_to(total, (1, LANES))
    sent(rcv_c, c_send, c_recv)
    for g in range(GROUPS):
        for s in range(n_steps):
            for d in range(1, steps[s][2]):
                share(g, s, d).wait_send()
    for part in range(len(mix_parts)):
        for d in range(1, n_tp):
            mix(part, d).wait_send()


def finish(stream_in, codes_in, recon_in, err_in, stream_ref, codes_ref, recon_ref, err_ref):
    stream_ref[...] = stream_in[...]
    codes_ref[...] = codes_in[...]
    keep, width = recon_ref.shape
    feats = width // LANES
    for c in range(feats):
        recon_ref[:, c * LANES:(c + 1) * LANES] = recon_in[pl.ds(c, keep, stride=feats), :].astype(BF16)
    for r in range(keep):
        err_ref[r] = err_in[r, 0]


def shards(attn_out, w_out, resid_in, positions, w_enc, b_enc, dec_norm, b_dec):
    n_tp = lax.axis_size("tp")
    n_lat = lax.axis_size("lat")
    n_dev = n_tp * n_lat
    rows, depth = attn_out.shape
    own_rows, width = resid_in.shape
    sel = positions.shape[0]
    lats = w_enc.shape[1]
    keep = sel // n_dev
    feats = width // LANES
    rg = feats // GROUPS * sel
    n_sem = GROUPS * sum(radix - 1 for _, _, radix in digits(n_tp, n_lat))
    vmem = pl.BlockSpec(memory_space=pltpu.VMEM)
    hbm = pl.BlockSpec(memory_space=pl.ANY)
    dma = pltpu.SemaphoreType.DMA
    made = pl.pallas_call(
        functools.partial(kernel, n_tp, n_lat),
        out_shape=(
            jax.ShapeDtypeStruct((own_rows, width), BF16),
            jax.ShapeDtypeStruct((sel, lats), BF16),
            jax.ShapeDtypeStruct((keep * feats, LANES), F32),
            jax.ShapeDtypeStruct((keep, LANES), F32),
        ),
        in_specs=[vmem] * 6 + [hbm] * 2,
        out_specs=(vmem,) * 4,
        scratch_shapes=[
            pltpu.VMEM((depth, width), BF16),
            pltpu.VMEM((width, lats), BF16),
            pltpu.VMEM((rows + sel + own_rows, depth), BF16),
            pltpu.VMEM((sel, own_rows), BF16),
            pltpu.VMEM((GROUPS * rg, LANES), F32),
            pltpu.VMEM((GROUPS * rg, LANES), BF16),
            pltpu.VMEM((GROUPS, rg, LANES), BF16),
            pltpu.VMEM((GROUPS, rg, LANES), BF16),
            pltpu.VMEM((GROUPS, rg, LANES), BF16),
            pltpu.VMEM((rows, width), BF16),
            pltpu.VMEM((n_tp - 1, own_rows, width), BF16),
            pltpu.VMEM((own_rows, width), F32),
            pltpu.VMEM((sel, lats), F32),
            pltpu.VMEM((sel, lats), BF16),
            pltpu.VMEM((keep, feats, LANES), F32),
            dma((2 * GROUPS,)),
            dma((8,)),
            dma((n_sem,)), dma((n_sem,)),
            dma((n_sem,)), dma((n_sem,)),
            dma((n_sem,)), dma((n_sem,)),
            dma((2 * (n_tp - 1),)), dma((2 * (n_tp - 1),)),
        ],
        compiler_params=pltpu.CompilerParams(
            collective_id=0, has_side_effects=True, vmem_limit_bytes=57 * 1024 * 1024
        ),
        cost_estimate=pl.CostEstimate(
            flops=2 * (2 * sel * width * lats + (rows + sel + own_rows) * depth * width),
            bytes_accessed=2 * (w_out.size + w_enc.size),
            transcendentals=0,
        ),
    )(
        positions.reshape(1, sel),
        attn_out,
        resid_in,
        b_enc.reshape(1, lats),
        dec_norm.reshape(1, lats),
        b_dec.reshape(feats, LANES),
        w_out,
        w_enc,
    )
    smem = pl.BlockSpec(memory_space=pltpu.SMEM)
    return pl.pallas_call(
        finish,
        out_shape=(
            jax.ShapeDtypeStruct((own_rows, width), BF16),
            jax.ShapeDtypeStruct((sel, lats), BF16),
            jax.ShapeDtypeStruct((keep, width), BF16),
            jax.ShapeDtypeStruct((keep,), F32),
        ),
        in_specs=[vmem] * 3 + [smem],
        out_specs=(vmem,) * 3 + (smem,),
    )(*made)


def solution(mesh):
    placed = (
        P("lat", "tp"),
        P("tp", None),
        P(("lat", "tp"), None),
        P(),
        P(None, ("tp", "lat")),
        P(("tp", "lat")),
        P(("tp", "lat")),
        P(),
    )
    return jax.shard_map(
        shards,
        mesh=mesh,
        in_specs=placed,
        out_specs=(
            P(("lat", "tp"), None),
            P(None, ("tp", "lat")),
            P(("tp", "lat"), None),
            P(("tp", "lat")),
        ),
        check_vma=False,
    )
```

```python
import functools

import jax
import jax.numpy as jnp
from jax import lax
from jax.experimental import pallas as pl
from jax.experimental.pallas import tpu as pltpu
from jax.sharding import PartitionSpec as P

GROUPS = 2
LANES = 128
F32 = jnp.float32
BF16 = jnp.bfloat16
MESH = pl.DeviceIdType.MESH


def log2(n):
    return n.bit_length() - 1


def digits(n_tp, n_lat):
    tp_bits, lat_bits = log2(n_tp), log2(n_lat)
    out = [("lat", 0, 2)] if lat_bits else []
    out += [("tp", b, 1 << min(2, tp_bits - b)) for b in range(0, tp_bits, 2)]
    out += [("lat", b, 1 << min(2, lat_bits - b)) for b in range(1, lat_bits, 2)]
    return out


def kernel(n_tp, n_lat, pos_ref, attn_ref, resid_ref, b_enc_ref, norm_ref, bdec_ref, w_out_hbm, w_enc_hbm,
           stream_ref, codes_ref, recon_ref, err_ref,
           w_out, w_enc, lhs, pick_own, acc, pk, snd, rcv_a, rcv_c, mix_snd, mix_rcv, mix_own, pre, cperm, mine,
           in_sem, enc_sem, a_send, a_recv, g_send, g_recv, c_send, c_recv, m_send, m_recv):
    ids = {"tp": lax.axis_index("tp"), "lat": lax.axis_index("lat")}
    n_dev = n_tp * n_lat
    rows, depth = attn_ref.shape
    own_rows, width = resid_ref.shape
    sel = pos_ref.shape[1]
    cg = width // LANES // GROUPS
    rg = cg * sel
    steps = digits(n_tp, n_lat)
    n_steps = len(steps)
    digit = [lax.rem(lax.div(ids[axis], 1 << low), radix) for axis, low, radix in steps]
    sizes = [rg]
    for axis, low, radix in steps:
        sizes.append(sizes[-1] // radix)
    offs = [0]
    sem_at = [0]
    for s in range(n_steps):
        offs.append(offs[-1] + (steps[s][2] - 1) * sizes[s + 1])
        sem_at.append(sem_at[-1] + steps[s][2] - 1)
    start = [0]
    for s in range(n_steps):
        start.append(start[-1] + digit[s] * sizes[s + 1])

    def towards(s, d):
        return lax.rem(digit[s] + d, steps[s][2])

    def peer(s, d):
        axis, low, radix = steps[s]
        return {axis: ids[axis] + (towards(s, d) - digit[s]) * (1 << low)}

    core = digit[0]
    half_cols = cg * LANES // 2

    def piece(g, which):
        h = 1 - core if which == 0 else core
        return pl.multiple_of(g * cg * LANES + h * half_cols, half_cols)

    def load(g, which):
        cols = pl.ds(piece(g, which), half_cols)
        return pltpu.make_async_copy(w_out_hbm.at[:, cols], w_out.at[:, cols], in_sem.at[which * GROUPS + g])

    for g in range(GROUPS):
        load(g, 0).start()
        load(g, 1).start()
    n_enc = enc_sem.shape[0]
    enc_rows = width // n_enc
    enc_loads = [
        pltpu.make_async_copy(w_enc_hbm.at[pl.ds(i * enc_rows, enc_rows), :], w_enc.at[pl.ds(i * enc_rows, enc_rows), :], enc_sem.at[i])
        for i in range(n_enc)
    ]

    barrier = pltpu.get_barrier_semaphore()
    mix_peer = lambda d: lax.rem(ids["tp"] + d, n_tp)
    peers = [peer(s, d) for s in range(n_steps) if steps[s][0] == "lat" for d in range(1, steps[s][2])]
    peers += [{"tp": mix_peer(d)} for d in range(1, n_tp)]
    for one in peers:
        pl.semaphore_signal(barrier, inc=1, device_id=one, device_id_type=MESH)

    base = ids["lat"] * rows
    hot = (lax.broadcasted_iota(jnp.int32, (rows, sel), 0) + base == pos_ref[...]).astype(BF16)
    lhs[0:rows, :] = attn_ref[...]
    lhs[rows:rows + sel, :] = lax.dot_general(hot, attn_ref[...], (((0,), (0,)), ((), ())), preferred_element_type=F32).astype(BF16)
    lhs[rows + sel:rows + sel + own_rows, :] = attn_ref[pl.ds(pl.multiple_of(ids["tp"] * own_rows, own_rows), own_rows), :]
    base = (ids["lat"] * n_tp + ids["tp"]) * own_rows
    hot = (lax.broadcasted_iota(jnp.int32, (own_rows, sel), 0) + base == pos_ref[...]).astype(BF16)
    eye = (lax.broadcasted_iota(jnp.int32, (own_rows, own_rows), 0) == lax.broadcasted_iota(jnp.int32, (own_rows, own_rows), 1)).astype(BF16)
    pick_own[...] = lax.dot_general(hot, eye, (((0,), (0,)), ((), ())), preferred_element_type=F32).astype(BF16)

    def span(at, size):
        return pl.ds(pl.multiple_of(at, size), size)

    def exchange(rcv, send_sem, recv_sem, g, s, d):
        at = pl.ds(offs[s] + (d - 1) * sizes[s + 1], sizes[s + 1])
        sem = g * sem_at[-1] + sem_at[s] + d - 1
        return pltpu.make_async_remote_copy(
            src_ref=snd.at[g, at, :],
            dst_ref=rcv.at[g, at, :],
            send_sem=send_sem.at[sem],
            recv_sem=recv_sem.at[sem],
            device_id=peer(s, d),
            device_id_type=MESH,
        )

    tile = min(512, half_cols)
    per = tile // LANES

    def project(g, which):
        load(g, which).wait()
        if g == GROUPS - 1 and which == 0:
            for one in enc_loads:
                one.start()
        first = piece(g, which)

        def body(i, _):
            cols = pl.ds(pl.multiple_of(first + i * tile, tile), tile)
            out = jnp.dot(lhs[...], w_out[:, cols], preferred_element_type=F32)
            mix_snd[:, cols] = out[0:rows].astype(BF16)
            mix_own[:, cols] = out[rows + sel:]
            part = out[rows:rows + sel] + jnp.dot(pick_own[...], resid_ref[:, cols], preferred_element_type=F32)
            for k in range(per):
                block = part[:, k * LANES:(k + 1) * LANES]
                at = (i * per + k) * sel
                if which == 0:
                    snd[g, pl.ds(pl.multiple_of(at, sel), sel), :] = block.astype(BF16)
                else:
                    acc[pl.ds(pl.multiple_of(g * rg + core * (rg // 2) + at, sel), sel), :] = block
            return 0

        lax.fori_loop(0, half_cols // tile, body, 0, unroll=True)
        if which == 0:
            if g == 0:
                pl.semaphore_wait(barrier, len(peers))
            exchange(rcv_a, a_send, a_recv, g, 0, 1).start()

    def take(rcv, send_sem, recv_sem, last, g, s):
        radix = steps[s][2]
        for d in range(1, radix):
            exchange(rcv, send_sem, recv_sem, g, s, d).wait_recv()

        def total(at, size):
            out = acc[span(g * rg + start[s + 1] + at, size), :]
            for d in range(1, radix):
                out = out + rcv[g, span(offs[s] + (d - 1) * sizes[s + 1] + at, size), :].astype(F32)
            return out

        if s + 1 == n_steps:
            last(g, total(0, sizes[s + 1]))
            return
        size = sizes[s + 2]
        for d in range(1, steps[s + 1][2]):
            snd[g, pl.ds(offs[s + 1] + (d - 1) * size, size), :] = total(towards(s + 1, d) * size, size).astype(BF16)
            exchange(rcv, send_sem, recv_sem, g, s + 1, d).start()
        acc[span(g * rg + start[s + 2], size), :] = total(digit[s + 1] * size, size)

    def sent(rcv, send_sem, recv_sem):
        for g in range(GROUPS):
            for s in range(n_steps):
                for d in range(1, steps[s][2]):
                    exchange(rcv, send_sem, recv_sem, g, s, d).wait_send()

    def share(g, s, d):
        at = span(g * rg + start[s + 1], sizes[s + 1])
        sem = g * sem_at[-1] + sem_at[s] + d - 1
        return pltpu.make_async_remote_copy(
            src_ref=pk.at[at, :],
            dst_ref=pk.at[at, :],
            send_sem=g_send.at[sem],
            recv_sem=g_recv.at[sem],
            device_id=peer(s, d),
            device_id_type=MESH,
        )

    def share_start(g, s):
        for d in range(1, steps[s][2]):
            share(g, s, d).start()

    def share_take(g, s):
        for d in range(1, steps[s][2]):
            share(g, s, d).wait_recv()

    def own_rows_done(g, total):
        pk[span(g * rg + start[n_steps], sizes[n_steps]), :] = total.astype(BF16)
        share_start(g, n_steps - 1)

    n_tile = min(256, pre.shape[1])

    def encode(g, at, size):
        count = size // sel
        first = g * cg + lax.div(at, sel)
        parts = []
        for k in range(count):
            ct = first + k
            block = pk[pl.ds(pl.multiple_of(ct * sel, sel), sel), :].astype(F32)
            acc[pl.ds(pl.multiple_of(ct * sel, sel), sel), :] = block
            parts.append((block - bdec_ref[pl.ds(ct, 1), :]).astype(BF16))
        left = jnp.concatenate(parts, axis=1)
        deep = pl.ds(pl.multiple_of(first * LANES, count * LANES), count * LANES)

        def body(i, _):
            cols = pl.ds(pl.multiple_of(i * n_tile, n_tile), n_tile)
            pre[:, cols] += jnp.dot(left, w_enc[deep, cols], preferred_element_type=F32)
            return 0

        lax.fori_loop(0, pre.shape[1] // n_tile, body, 0, unroll=True)

    mix_parts = (pl.ds(0, width // 4), pl.ds(width // 4, width - width // 4))

    def mix(part, d):
        to = mix_peer(d)
        sem = part * (n_tp - 1) + d - 1
        return pltpu.make_async_remote_copy(
            src_ref=mix_snd.at[pl.ds(pl.multiple_of(to * own_rows, own_rows), own_rows), mix_parts[part]],
            dst_ref=mix_rcv.at[d - 1, :, mix_parts[part]],
            send_sem=m_send.at[sem],
            recv_sem=m_recv.at[sem],
            device_id={"tp": to},
            device_id_type=MESH,
        )

    def mix_start(part):
        for d in range(1, n_tp):
            mix(part, d).start()

    def mix_early(t):
        if t == GROUPS:
            mix_start(0)

    def wave(ops, after=None):
        for t in range(len(ops) + GROUPS - 1):
            for g in reversed(range(GROUPS)):
                if 0 <= t - g < len(ops):
                    ops[t - g](g)
            if after is not None:
                after(t)

    def encode_near(g):
        share_take(g, 1)
        share_start(g, 0)
        if g == GROUPS - 1:
            mix_start(1)
        if g == 0:
            for one in enc_loads:
                one.wait()
        encode(g, start[1], rg // 2)

    def encode_far(g):
        share_take(g, 0)
        encode(g, (1 - core) * (rg // 2), rg // 2)

    def pass_on(g, s):
        if g == GROUPS - 1 and s == n_steps - 1:
            sent(rcv_a, a_send, a_recv)
        share_take(g, s)
        share_start(g, s - 1)

    pre[...] = jnp.zeros_like(pre)
    take_a = functools.partial(take, rcv_a, a_send, a_recv, own_rows_done)
    for g in range(GROUPS):
        project(g, 0)
        if g > 0:
            take_a(g - 1, 0)
        project(g, 1)

    def take_last(g):
        if g == GROUPS - 1:
            take_a(g, 0)

    ops = [take_last] + [functools.partial(take_a, s=s) for s in range(1, n_steps)]
    ops += [functools.partial(pass_on, s=s) for s in reversed(range(2, n_steps))]
    ops += [encode_near, encode_far]
    wave(ops, mix_early)

    codes = (jnp.maximum(pre[...] + b_enc_ref[...], 0.0) * norm_ref[...]).astype(BF16)
    codes_ref[...] = codes

    keep = sel // n_dev
    me = ids["tp"] * n_lat + ids["lat"]
    for r in range(keep):
        mine[r] = acc[pl.ds(me * keep + r, width // LANES, stride=sel), :]

    q = lax.broadcasted_iota(jnp.int32, (sel, sel), 0)
    row = lax.rem(q, keep)
    for s, (axis, low, radix) in enumerate(steps):
        weight = keep * (1 << low) * (n_lat if axis == "tp" else 1)
        row = row + lax.rem(lax.div(q, sizes[s + 1] // cg), radix) * weight
    turn = (row == lax.broadcasted_iota(jnp.int32, (sel, sel), 1)).astype(BF16)
    cperm[...] = jnp.dot(turn, codes, preferred_element_type=F32).astype(BF16)
    d_tile = min(256, cg * LANES)
    d_per = d_tile // LANES

    d_count = cg * LANES // d_tile

    def decode(g, low, high):
        left = cperm[...]

        def body(i, _):
            at = pl.ds(pl.multiple_of(g * cg * LANES + i * d_tile, d_tile), d_tile)
            out = lax.dot_general(left, w_enc[at, :], (((1,), (1,)), ((), ())), preferred_element_type=F32)
            for k in range(d_per):
                acc[pl.ds(g * rg + i * d_per + k, sel, stride=cg), :] = out[:, k * LANES:(k + 1) * LANES]
            return 0

        lax.fori_loop(low, high, body, 0, unroll=True)
        if high < d_count:
            return
        half = rg // 2
        snd[g, pl.ds(0, half), :] = acc[span(g * rg + (1 - core) * half, half), :].astype(BF16)
        exchange(rcv_c, c_send, c_recv, g, 0, 1).start()

    sums = [None] * keep

    def score(g, total):
        for r in range(keep):
            full = total[r * cg:(r + 1) * cg] + bdec_ref[g * cg:(g + 1) * cg, :]
            recon_ref[r * (width // LANES) + g * cg:r * (width // LANES) + (g + 1) * cg, :] = full
            off = full - mine[r, g * cg:(g + 1) * cg, :]
            sums[r] = off * off if sums[r] is None else sums[r] + off * off

    def keep_stream():
        for part in range(len(mix_parts)):
            for d in range(1, n_tp):
                mix(part, d).wait_recv()

        def body(i, _):
            cols = pl.ds(pl.multiple_of(i * 1024, 1024), 1024)
            total = mix_own[:, cols]
            for d in range(1, n_tp):
                total = total + mix_rcv[d - 1, :, cols].astype(F32)
            stream_ref[:, cols] = (resid_ref[:, cols].astype(F32) + total).astype(BF16)
            return 0

        lax.fori_loop(0, width // 1024, body, 0)

    take_c = functools.partial(take, rcv_c, c_send, c_recv, score)
    decode(0, 0, d_count)
    for g in range(1, GROUPS):
        decode(g, 0, d_count // 2)
        take_c(g - 1, 0)
        decode(g, d_count // 2, d_count)
    take_c(GROUPS - 1, 0)
    for s in range(1, n_steps):
        if s == n_steps - 1:
            keep_stream()
        for g in range(GROUPS):
            take_c(g, s)
    for r in range(keep):
        total = jnp.sum(jnp.sum(sums[r], axis=0, keepdims=True), axis=1, keepdims=True) / width
        err_ref[r:r + 1, :] = jnp.broadcast_to(total, (1, LANES))
    sent(rcv_c, c_send, c_recv)
    for g in range(GROUPS):
        for s in range(n_steps):
            for d in range(1, steps[s][2]):
                share(g, s, d).wait_send()
    for part in range(len(mix_parts)):
        for d in range(1, n_tp):
            mix(part, d).wait_send()


def finish(stream_in, codes_in, recon_in, err_in, stream_ref, codes_ref, recon_ref, err_ref):
    stream_ref[...] = stream_in[...]
    codes_ref[...] = codes_in[...]
    keep, width = recon_ref.shape
    feats = width // LANES
    for c in range(feats):
        recon_ref[:, c * LANES:(c + 1) * LANES] = recon_in[pl.ds(c, keep, stride=feats), :].astype(BF16)
    for r in range(keep):
        err_ref[r] = err_in[r, 0]


def shards(attn_out, w_out, resid_in, positions, w_enc, b_enc, dec_norm, b_dec):
    n_tp = lax.axis_size("tp")
    n_lat = lax.axis_size("lat")
    n_dev = n_tp * n_lat
    rows, depth = attn_out.shape
    own_rows, width = resid_in.shape
    sel = positions.shape[0]
    lats = w_enc.shape[1]
    keep = sel // n_dev
    feats = width // LANES
    rg = feats // GROUPS * sel
    n_sem = GROUPS * sum(radix - 1 for _, _, radix in digits(n_tp, n_lat))
    vmem = pl.BlockSpec(memory_space=pltpu.VMEM)
    hbm = pl.BlockSpec(memory_space=pl.ANY)
    dma = pltpu.SemaphoreType.DMA
    made = pl.pallas_call(
        functools.partial(kernel, n_tp, n_lat),
        out_shape=(
            jax.ShapeDtypeStruct((own_rows, width), BF16),
            jax.ShapeDtypeStruct((sel, lats), BF16),
            jax.ShapeDtypeStruct((keep * feats, LANES), F32),
            jax.ShapeDtypeStruct((keep, LANES), F32),
        ),
        in_specs=[vmem] * 6 + [hbm] * 2,
        out_specs=(vmem,) * 4,
        scratch_shapes=[
            pltpu.VMEM((depth, width), BF16),
            pltpu.VMEM((width, lats), BF16),
            pltpu.VMEM((rows + sel + own_rows, depth), BF16),
            pltpu.VMEM((sel, own_rows), BF16),
            pltpu.VMEM((GROUPS * rg, LANES), F32),
            pltpu.VMEM((GROUPS * rg, LANES), BF16),
            pltpu.VMEM((GROUPS, rg, LANES), BF16),
            pltpu.VMEM((GROUPS, rg, LANES), BF16),
            pltpu.VMEM((GROUPS, rg, LANES), BF16),
            pltpu.VMEM((rows, width), BF16),
            pltpu.VMEM((n_tp - 1, own_rows, width), BF16),
            pltpu.VMEM((own_rows, width), F32),
            pltpu.VMEM((sel, lats), F32),
            pltpu.VMEM((sel, lats), BF16),
            pltpu.VMEM((keep, feats, LANES), F32),
            dma((2 * GROUPS,)),
            dma((8,)),
            dma((n_sem,)), dma((n_sem,)),
            dma((n_sem,)), dma((n_sem,)),
            dma((n_sem,)), dma((n_sem,)),
            dma((2 * (n_tp - 1),)), dma((2 * (n_tp - 1),)),
        ],
        compiler_params=pltpu.CompilerParams(
            collective_id=0, has_side_effects=True, vmem_limit_bytes=57 * 1024 * 1024
        ),
        cost_estimate=pl.CostEstimate(
            flops=2 * (2 * sel * width * lats + (rows + sel + own_rows) * depth * width),
            bytes_accessed=2 * (w_out.size + w_enc.size),
            transcendentals=0,
        ),
    )(
        positions.reshape(1, sel),
        attn_out,
        resid_in,
        b_enc.reshape(1, lats),
        dec_norm.reshape(1, lats),
        b_dec.reshape(feats, LANES),
        w_out,
        w_enc,
    )
    smem = pl.BlockSpec(memory_space=pltpu.SMEM)
    return pl.pallas_call(
        finish,
        out_shape=(
            jax.ShapeDtypeStruct((own_rows, width), BF16),
            jax.ShapeDtypeStruct((sel, lats), BF16),
            jax.ShapeDtypeStruct((keep, width), BF16),
            jax.ShapeDtypeStruct((keep,), F32),
        ),
        in_specs=[vmem] * 3 + [smem],
        out_specs=(vmem,) * 3 + (smem,),
    )(*made)


def solution(mesh):
    placed = (
        P("lat", "tp"),
        P("tp", None),
        P(("lat", "tp"), None),
        P(),
        P(None, ("tp", "lat")),
        P(("tp", "lat")),
        P(("tp", "lat")),
        P(),
    )
    return jax.shard_map(
        shards,
        mesh=mesh,
        in_specs=placed,
        out_specs=(
            P(("lat", "tp"), None),
            P(None, ("tp", "lat")),
            P(("tp", "lat"), None),
            P(("tp", "lat")),
        ),
        check_vma=False,
    )
```
